128 devices in a mesh: cfg: 2 (over core), blk: 8 (over x_lo, y), sp: 8 (over z, x_hi).
Axes of the slice: x: 4 (x_hi: 2, x_lo: 2; x = x_hi * 2 + x_lo), y: 4, z: 4, core: 2. Of those that a mesh axis runs over, the one named last changes fastest.
Arguments:
- qkv: bfloat16 [2, 16, 512, 9216], P('cfg', 'blk', 'sp'), may hold values from -130 to 130
- residual: bfloat16 [2, 16, 512, 3072], P('cfg', 'blk', 'sp'), may hold values from -4 to 4
- text_kv: bfloat16 [2, 256, 2, 24, 128], P('cfg'), may hold values from -16 to 16
- text_len: int32 [2], P('cfg'), may hold values from 128 to 256
- text_keep: int32 [2, 256], P('cfg'), may hold values 0 or 1
- attn_gate: float32 [2, 3072], P('cfg'), may hold values from 1 to 3
- w_out: bfloat16 [3072, 3072], replicated, may hold values from -0.109375 to 0.109375
- final_mod: float32 [2, 2, 3072], P('cfg'), may hold values from -3 to 3
- w_final: bfloat16 [3072, 64], replicated, may hold values from -0.109375 to 0.109375
- noisy: float32 [16, 512, 64], P('blk', 'sp'), may hold values from -6 to 6
- conv_weight: bfloat16 [3, 16, 512], replicated, may hold values from -0.875 to 0.875
- conv_bias: float32 [512], replicated, may hold values from -3 to 3
Outputs:
- velocity: float32 [16, 512, 64], P('blk', 'sp')
- decoded: bfloat16 [16, 512, 4, 512], P('blk', 'sp', 'cfg')
The draws below stay inside these ranges and needn't reach their ends.
All inputs are finite; a program needn't handle non-finite values. No bound on the sum of `text_keep` on one device may be relied on, other than what follows from the above.
Results may differ from the reference program's by a relative error of at most 0.012.
Values may be sent and summed in bfloat16 or wider, within the bound.
A program may use at most 128 MiB of HBM per device.

```python
import math
import jax
import jax.numpy as jnp
from jax import lax

D = 3072
H = 24
HD = 128
TXT = 256
LAT = 16
CH = 512
FRAMES = 16
PIX = 512


def draw_qkv(key, part):
    key = jax.random.fold_in(key, 11)
    base = jax.random.truncated_normal(key, -6.0, 6.0, (2, FRAMES, PIX, 3, D), jnp.float32)
    scales = jnp.array([1.5, 1.5, 1.0], jnp.float32)
    values = base * scales[None, None, None, :, None]
    return values.reshape(2, FRAMES, PIX, 3 * D).astype(jnp.bfloat16)


def with_ends(entries, own_key, low, largest):
    longest = entries.shape.index(max(entries.shape))
    spots = []
    for shift in (0, 1):
        where = [jax.random.randint(jax.random.fold_in(own_key, axis), (), 0, length) for axis, length in enumerate(entries.shape)]
        where[longest] = (where[longest] + shift) % entries.shape[longest]
        spots.append(tuple(where))
    return entries.at[spots[0]].set(low).at[spots[1]].set(largest)


def block_levels(stream_key, dims, shards, smallest, top_value):
    def one(dim, shards_of):
        draws = jax.random.uniform(jax.random.fold_in(jax.random.fold_in(stream_key, 6), dim), (shards_of,), jnp.float32, smallest / len(shards), top_value / len(shards))
        return jnp.repeat(jnp.exp(draws), dims[dim] // shards_of).reshape((-1,) + (1,) * (len(dims) - dim - 1))

    loudness = one(*shards[0])
    for cut in shards[1:]:
        loudness = loudness * one(*cut)
    return loudness


def noise(key, extent, scale, reach, pieces=(), held_as=jnp.bfloat16):
    values = scale * jax.random.normal(key, extent, jnp.float32)
    if pieces:
        values = values * block_levels(key, extent, pieces, -0.22, 0.18)
    return jnp.clip(values, -reach, reach).astype(held_as)


def setup_inputs(seed: int = 0) -> dict:
    streams_of = jax.random.split(jax.random.key(seed), 13)
    qkv = draw_qkv(jax.random.fold_in(streams_of[12], 71), 0)
    residual = noise(streams_of[1], (2, FRAMES, PIX, D), 0.3, 4.0, ((0, 2), (1, 8), (2, 8)))
    text_kv = noise(streams_of[2], (2, TXT, 2, H, HD), 3.0, 16.0, ((0, 2),))
    text_len = jax.random.randint(streams_of[3], (2,), TXT // 2, TXT + 1).astype(jnp.int32)
    text_keep = with_ends((jax.random.randint(streams_of[4], (2, TXT), 0, 2) < 1).astype(jnp.int32), jax.random.fold_in(streams_of[4], 1), 0, 1)
    attn_gate = jnp.clip(1.0 + 2.0 * jax.random.uniform(streams_of[5], (2, D), jnp.float32) ** block_levels(streams_of[5], (2, D), ((0, 2),), -0.2, 0.2), 1.0, 3.0)
    w_out = noise(streams_of[6], (D, D), D ** -0.5, 0.109375)
    final_mod = noise(streams_of[7], (2, 2, D), 0.5, 3.0, ((0, 2),), jnp.float32)
    w_final = noise(streams_of[8], (D, 4 * LAT), D ** -0.5, 0.109375)
    noisy = noise(streams_of[9], (FRAMES, PIX, 4 * LAT), 1.0, 6.0, ((0, 8), (1, 8)), jnp.float32)
    conv_weight = noise(streams_of[10], (3, LAT, CH), (3 * LAT) ** -0.5, 0.875)
    conv_bias = noise(streams_of[11], (CH,), 0.5, 3.0, (), jnp.float32)
    return dict(qkv=qkv, residual=residual, text_kv=text_kv, text_len=text_len, text_keep=text_keep, attn_gate=attn_gate, w_out=w_out, final_mod=final_mod, w_final=w_final, noisy=noisy, conv_weight=conv_weight, conv_bias=conv_bias)


guidance_scale = 6.0
sigma_last = 0.125
vae_factor = 0.476986
norm_eps = 1e-06

def head_attention(queries, keys_all, values_all, key_mask):
    scores = jnp.dot(queries, keys_all.T, preferred_element_type=jnp.float32) / math.sqrt(HD)
    scores = jnp.where(key_mask[None, :], scores, -jnp.inf)
    row_max = lax.optimization_barrier(jnp.max(scores, axis=-1, keepdims=True))
    weights = jnp.where(key_mask[None, :], jnp.exp(scores - row_max), 0.0)
    row_sum = lax.optimization_barrier(jnp.sum(weights, axis=-1, keepdims=True))
    summed = jnp.dot(weights.astype(jnp.bfloat16), values_all, preferred_element_type=jnp.float32)
    return (summed / row_sum).astype(jnp.bfloat16)

def reference(qkv, residual, text_kv, text_len, text_keep, attn_gate, w_out, final_mod, w_final, noisy, conv_weight, conv_bias):
    seq_total = FRAMES * PIX
    predictions = []
    for guide_half in range(2):
        tokens_qkv = qkv[guide_half].reshape(seq_total, 3, H, HD)
        keys_all = jnp.concatenate([tokens_qkv[:, 1], text_kv[guide_half, :, 0]], axis=0)
        values_all = jnp.concatenate([tokens_qkv[:, 2], text_kv[guide_half, :, 1]], axis=0)
        position = jnp.arange(TXT, dtype=jnp.int32)
        text_mask = (position < text_len[guide_half]) & (text_keep[guide_half] == 1)
        key_mask = jnp.concatenate([jnp.ones((seq_total,), dtype=bool), text_mask])
        per_head = lax.map(lambda parts: head_attention(parts[0], parts[1], parts[2], key_mask), (jnp.swapaxes(tokens_qkv[:, 0], 0, 1), jnp.swapaxes(keys_all, 0, 1), jnp.swapaxes(values_all, 0, 1)))
        attended = jnp.swapaxes(per_head, 0, 1).reshape(seq_total, D)
        projected = jnp.dot(attended, w_out, preferred_element_type=jnp.float32)
        hidden = residual[guide_half].reshape(seq_total, D).astype(jnp.float32) + attn_gate[guide_half] * projected
        centered = hidden - lax.optimization_barrier(jnp.mean(hidden, axis=-1, keepdims=True))
        normed = centered * lax.rsqrt(lax.optimization_barrier(jnp.mean(centered * centered, axis=-1, keepdims=True)) + norm_eps)
        modulated = (normed * (1.0 + final_mod[guide_half, 1]) + final_mod[guide_half, 0]).astype(jnp.bfloat16)
        predictions.append(jnp.dot(modulated, w_final, preferred_element_type=jnp.float32))
    guided = predictions[1] + guidance_scale * (predictions[0] - predictions[1])
    velocity = guided.reshape(FRAMES, PIX, 4 * LAT)
    latent = ((noisy - sigma_last * velocity) / vae_factor).astype(jnp.bfloat16)
    pixel_grid = latent.reshape(FRAMES, PIX, LAT, 4).astype(jnp.float32)
    padded = jnp.concatenate([jnp.zeros((2, PIX, LAT, 4), jnp.float32), pixel_grid], axis=0)
    summed = jnp.zeros((FRAMES, PIX, 4, CH), jnp.float32) + conv_bias
    for offset in range(3):
        summed = summed + jnp.einsum('fpcx,co->fpxo', padded[offset:offset + FRAMES], conv_weight[offset].astype(jnp.float32))
    return (velocity, summed.astype(jnp.bfloat16))
```

```python
import functools
import math

import jax
import jax.numpy as jnp
from jax import lax
from jax.experimental import pallas as pl
from jax.experimental.pallas import tpu as pltpu
from jax.sharding import PartitionSpec as P

D = 3072
H = 24
HD = 128
G = 3
TXT = 256
ROWS = 128
QB = 256
MESH = pl.DeviceIdType.MESH
SCALE = math.log2(math.e) / math.sqrt(HD)
BF = jnp.bfloat16
F32 = jnp.float32

guidance_scale = 6.0
sigma_last = 0.125
vae_factor = 0.476986
norm_eps = 1e-06


def wait_bytes(ref, sem):
    pltpu.make_async_copy(ref, ref, sem).wait()


def body(
    qkv, residual, text, bias, gate, w_out, fmod, w_fin, noisy, conv_w, conv_b,
    velocity, decoded,
    qb, kv, ob, att, tb, mb, wo, res, wf, proj, mod, pb, lat, halo, acc, m_s, l_s,
    snd, rcv_q, rcv_k, rcv_v, ysnd, yrcv, dsnd, drcv, osnd, orcv, lsem, tsnd, trcv, psnd, prcv, hsnd, hrcv,
):
    c = lax.axis_index("cfg")
    b = lax.axis_index("blk")
    s = lax.axis_index("sp")
    xl = b // 4
    y = b % 4
    up = (y + 1) % 4
    dn = (y + 3) % 4
    opp = (y + 2) % 4
    to_up = (c, xl * 4 + up, s)
    to_dn = (c, xl * 4 + dn, s)
    to_core = (1 - c, b, s)
    moved = c != xl

    def peer(d):
        return (xl, c * 4 + y, d)

    def remote(src, dst, send, recv, dev):
        return pltpu.make_async_remote_copy(src, dst, send, recv, device_id=dev, device_id_type=MESH)

    fetch_w = pltpu.make_async_copy(w_out, wo, lsem.at[0])
    fetch_r = pltpu.make_async_copy(residual.at[0], res, lsem.at[1])
    fetch_f = pltpu.make_async_copy(w_fin, wf, lsem.at[2])

    bar = pltpu.get_barrier_semaphore()

    def sig(dev):
        pl.semaphore_signal(bar, inc=1, device_id=dev, device_id_type=MESH)

    sig(to_up)
    sig(to_dn)
    sig(to_core)
    for j in range(1, 8):
        sig(peer((s + j) % 8))

    @pl.when(moved)
    def _():
        sig(peer(s))

    @pl.when(b < 7)
    def _():
        sig((c, b + 1, s))

    @pl.when(b > 0)
    def _():
        sig((c, b - 1, s))

    count = 10 + jnp.where(moved, 1, 0) + jnp.where(b < 7, 1, 0) + jnp.where(b > 0, 1, 0)
    pl.semaphore_wait(bar, count)

    rcvs = (rcv_q, rcv_k, rcv_v)

    def send_head(h):
        for kind in (1, 2, 0):
            landing = qb.at[h, s] if kind == 0 else kv.at[h, y, xl, kind - 1, s]

            def piece(d):
                return qkv.at[0, :, :, pl.ds(pl.multiple_of(kind * D + (d * G + h) * HD, HD), HD)]

            def one(j, carry):
                d = (s + j) % 8
                remote(piece(d), landing, snd.at[h, kind], rcvs[kind].at[h], peer(d)).start()
                return carry

            lax.fori_loop(1, 8, one, 0)

            @pl.when(moved)
            def _():
                remote(piece(s), landing, snd.at[h, kind], rcvs[kind].at[h], peer(s)).start()

            @pl.when(jnp.logical_not(moved))
            def _():
                pltpu.make_async_copy(piece(s), landing, rcvs[kind].at[h]).start()

    def wait_head(h):
        wait_bytes(kv.at[h, y, c, 0], rcv_k.at[h])
        wait_bytes(kv.at[h, y, c, 1], rcv_v.at[h])
        wait_bytes(qb.at[h], rcv_q.at[h])

    def core_copy(h, i, yy):
        return remote(kv.at[h, yy, c], kv.at[h, yy, c], dsnd.at[h, i], drcv.at[h, i], to_core)

    def wait_core(h, i, yy):
        wait_bytes(kv.at[h, yy, 1 - c], drcv.at[h, i])

    def ring_copy(h, i, yy, part, dev):
        ref = kv.at[h, yy, c, part]
        return remote(ref, ref, ysnd.at[h, i], yrcv.at[h, i], dev)

    def wait_ring(h, i, yy, part):
        wait_bytes(kv.at[h, yy, c, part], yrcv.at[h, i])

    def send_own(h):
        ring_copy(h, 0, y, 0, to_up).start()
        ring_copy(h, 2, y, 1, to_dn).start()
        ring_copy(h, 1, y, 1, to_up).start()
        ring_copy(h, 3, y, 0, to_dn).start()
        core_copy(h, 0, y).start()

    text_own = pltpu.make_async_copy(text, tb.at[c], lsem.at[3])
    text_out = remote(text, tb.at[c], tsnd.at[0], trcv.at[0], to_core)
    mask_own = pltpu.make_async_copy(bias, mb.at[c], lsem.at[4])
    mask_out = remote(bias, mb.at[c], tsnd.at[1], trcv.at[1], to_core)

    send_head(0)
    text_own.start()
    text_out.start()
    mask_own.start()
    mask_out.start()
    send_head(1)
    send_head(2)
    fetch_w.start()
    fetch_r.start()
    fetch_f.start()

    text_own.wait()
    mask_own.wait()
    wait_bytes(tb.at[1 - c], trcv.at[0])
    wait_bytes(mb.at[1 - c], trcv.at[1])

    wait_head(0)
    send_own(0)

    def queries(h, u):
        return qb[h, pl.ds(2 * u, 2)].reshape(QB, HD)

    def scores(q, keys):
        return lax.dot_general(q, keys, (((1,), (1,)), ((), ())), preferred_element_type=F32)

    def weigh(weights, values):
        padded = jnp.concatenate([values, jnp.ones_like(values)], axis=1)
        return jnp.dot(weights.astype(BF), padded, preferred_element_type=F32)

    blocks = 1024 // QB

    def text_step(h):
        keys = tb[xl, h, 0]
        values = tb[xl, h, 1]
        added = mb[xl]
        for u in range(blocks):
            rows = pl.ds(u * QB, QB)
            sc = scores(queries(h, u), keys) + added[0:1]
            top = jnp.max(sc, axis=1, keepdims=True)
            out = weigh(jnp.exp2((sc - top) * SCALE), values)
            m_s[rows] = jnp.broadcast_to(top, (QB, HD))
            acc[rows] = out[:, :HD]
            l_s[rows] = out[:, HD:]

    def key_step(h, yy):
        keys = kv[h, yy, :, 0].reshape(2048, HD)
        values = kv[h, yy, :, 1].reshape(2048, HD)

        def finish(u, sc):
            rows = pl.ds(u * QB, QB)
            old = m_s[rows]
            new = jnp.maximum(old, jnp.max(sc, axis=1, keepdims=True))
            factor = jnp.exp2((old - new) * SCALE)
            out = weigh(jnp.exp2((sc - new[:, :1]) * SCALE), values)
            m_s[rows] = new
            acc[rows] = acc[rows] * factor + out[:, :HD]
            l_s[rows] = l_s[rows] * factor + out[:, HD:]

        now = scores(queries(h, 0), keys)
        for u in range(blocks):
            later = scores(queries(h, u + 1), keys) if u + 1 < blocks else None
            finish(u, now)
            now = later

    def project(h, first):
        wait_bytes(att.at[:, h], orcv.at[h])
        rows = jnp.concatenate([att[d, h].reshape(ROWS, HD) for d in range(8)], axis=1)

        def columns(n, carry):
            cols = pl.ds(pl.multiple_of(n * 512, 512), 512)
            weight = jnp.concatenate(
                [wo[pl.ds(pl.multiple_of((d * G + h) * HD, HD), HD), cols] for d in range(8)], axis=0
            )
            out = jnp.dot(rows, weight, preferred_element_type=F32)
            if first:
                proj[:, cols] = out
            else:
                proj[:, cols] += out
            return carry

        lax.fori_loop(0, D // 512, columns, 0)

    def send_back(h):
        ob[h] = (acc[...] / l_s[...]).astype(BF).reshape(8, 2, 64, HD)

        def one(j, carry):
            d = (s + j) % 8
            remote(ob.at[h, d], att.at[s, h], osnd.at[h], orcv.at[h], peer(d)).start()
            return carry

        lax.fori_loop(1, 8, one, 0)

        @pl.when(moved)
        def _():
            remote(ob.at[h, s], att.at[s, h], osnd.at[h], orcv.at[h], peer(s)).start()

        @pl.when(jnp.logical_not(moved))
        def _():
            pltpu.make_async_copy(ob.at[h, s], att.at[s, h], orcv.at[h]).start()

    def step(t, carry):
        h = t // 4
        p = t % 4
        yy = (y + p + p // 2 - 2 * (p // 3)) % 4

        @pl.when(p == 0)
        def _():
            text_step(h)

        @pl.when(p == 1)
        def _():
            wait_ring(h, 2, up, 1)
            ring_copy(h, 5, up, 1, to_dn).start()
            wait_ring(h, 0, dn, 0)
            ring_copy(h, 4, dn, 0, to_up).start()
            wait_ring(h, 3, up, 0)
            core_copy(h, 1, up).start()
            wait_ring(h, 1, dn, 1)
            core_copy(h, 2, dn).start()

            @pl.when(h < 2)
            def _():
                wait_head(h + 1)
                send_own(h + 1)

        @pl.when(p == 3)
        def _():
            wait_ring(h, 4, opp, 0)
            wait_ring(h, 5, opp, 1)
            core_copy(h, 3, opp).start()

        wait_core(h, p, yy)
        key_step(h, yy)

        @pl.when(p == 3)
        def _():
            send_back(h)

        @pl.when(t == 6)
        def _():
            fetch_w.wait()
            project(0, True)

        @pl.when(t == 10)
        def _():
            project(1, False)

        return carry

    lax.fori_loop(0, 12, step, 0)
    project(2, False)

    fetch_r.wait()
    fetch_f.wait()

    def norm(n, carry):
        rows = pl.ds(pl.multiple_of(n * 32, 32), 32)
        shown = res[n // 2, pl.ds(pl.multiple_of((n % 2) * 32, 32), 32)].astype(F32)
        hidden = shown + gate[...] * proj[rows]
        centered = hidden - jnp.mean(hidden, axis=1, keepdims=True)
        normed = centered * lax.rsqrt(jnp.mean(centered * centered, axis=1, keepdims=True) + norm_eps)
        mod[rows] = (normed * (1.0 + fmod[0, 1:2]) + fmod[0, 0:1]).astype(BF)
        return carry

    lax.fori_loop(0, 4, norm, 0)
    pb[c] = jnp.dot(mod[...], wf[...], preferred_element_type=F32)
    pred_out = remote(pb.at[c], pb.at[c], psnd, prcv, to_core)
    pred_out.start()
    wait_bytes(pb.at[1 - c], prcv)
    uncond = pb[1]
    guided = uncond + guidance_scale * (pb[0] - uncond)
    velocity[...] = guided
    lat[...] = ((noisy[...] - sigma_last * guided) / vae_factor).astype(BF)

    @pl.when(b < 7)
    def _():
        remote(lat, halo, hsnd, hrcv, (c, b + 1, s)).start()

    @pl.when(b == 0)
    def _():
        halo[...] = jnp.zeros_like(halo)

    @pl.when(b > 0)
    def _():
        wait_bytes(halo, hrcv)

    before = halo[...]
    here = lat[...]
    across = jnp.concatenate([before[64:], here[:64]], axis=0)
    entry = lax.broadcasted_iota(jnp.int32, (64, 48), 0)
    place = lax.broadcasted_iota(jnp.int32, (64, 48), 1)
    for i in range(2):
        taps = jnp.zeros((ROWS, 48), F32)
        for t, frames in enumerate((before, across, here)):
            chosen = (entry == 4 * (place - 16 * t) + 2 * c + i) & (place >= 16 * t) & (place < 16 * t + 16)
            taps = taps + jnp.dot(frames, jnp.where(chosen, 1.0, 0.0).astype(BF), preferred_element_type=F32)
        out = jnp.dot(taps.astype(BF), conv_w[...], preferred_element_type=F32) + conv_b[...]
        decoded[:, i * 512 : (i + 1) * 512] = out.astype(BF)

    for h in range(3):
        for kind in range(3):
            wait_bytes(qb.at[h, pl.ds(0, 7)], snd.at[h, kind])

            @pl.when(moved)
            def _():
                wait_bytes(qb.at[h, 0], snd.at[h, kind])

        for i in range(6):
            wait_bytes(kv.at[h, y, c, 0], ysnd.at[h, i])
        for i in range(4):
            wait_bytes(kv.at[h, y, c], dsnd.at[h, i])
        wait_bytes(ob.at[h, pl.ds(0, 7)], osnd.at[h])

        @pl.when(moved)
        def _():
            wait_bytes(ob.at[h, 0], osnd.at[h])

    wait_bytes(tb.at[c], tsnd.at[0])
    wait_bytes(mb.at[c], tsnd.at[1])
    wait_bytes(pb.at[c], psnd)

    @pl.when(b < 7)
    def _():
        wait_bytes(lat, hsnd)


def shards(qkv, residual, text_kv, text_len, text_keep, attn_gate, w_out, final_mod, w_final, noisy, conv_weight, conv_bias):
    text_mask = (jnp.arange(TXT, dtype=jnp.int32) < text_len[0]) & (text_keep[0] == 1)
    bias = jnp.broadcast_to(jnp.where(text_mask, 0.0, -1e30).astype(F32)[None], (8, TXT))
    text = lax.dynamic_slice_in_dim(text_kv[0], lax.axis_index("sp") * G, G, axis=2)
    text = jnp.transpose(text, (2, 1, 0, 3))
    hbm = pl.BlockSpec(memory_space=pl.ANY)
    vmem = pl.BlockSpec(memory_space=pltpu.VMEM)
    dma = pltpu.SemaphoreType.DMA
    velocity, decoded = pl.pallas_call(
        body,
        out_shape=(
            jax.ShapeDtypeStruct((ROWS, 64), F32),
            jax.ShapeDtypeStruct((ROWS, 1024), BF),
        ),
        in_specs=[hbm, hbm, vmem, vmem, vmem, hbm, vmem, hbm, vmem, vmem, vmem],
        out_specs=(vmem, vmem),
        scratch_shapes=[
            pltpu.VMEM((G, 8, 2, 64, HD), BF),
            pltpu.VMEM((G, 4, 2, 2, 8, 2, 64, HD), BF),
            pltpu.VMEM((G, 8, 2, 64, HD), BF),
            pltpu.VMEM((8, G, 2, 64, HD), BF),
            pltpu.VMEM((2, G, 2, TXT, HD), BF),
            pltpu.VMEM((2, 8, TXT), F32),
            pltpu.VMEM((D, D), BF),
            pltpu.VMEM((2, 64, D), BF),
            pltpu.VMEM((D, 64), BF),
            pltpu.VMEM((ROWS, D), F32),
            pltpu.VMEM((ROWS, D), BF),
            pltpu.VMEM((2, ROWS, 64), F32),
            pltpu.VMEM((ROWS, 64), BF),
            pltpu.VMEM((ROWS, 64), BF),
            pltpu.VMEM((1024, HD), F32),
            pltpu.VMEM((1024, HD), F32),
            pltpu.VMEM((1024, HD), F32),
            dma((G, 3)),
            dma((G,)),
            dma((G,)),
            dma((G,)),
            dma((G, 6)),
            dma((G, 6)),
            dma((G, 4)),
            dma((G, 4)),
            dma((G,)),
            dma((G,)),
            dma((5,)),
            dma((2,)),
            dma((2,)),
            dma,
            dma,
            dma,
            dma,
        ],
        compiler_params=pltpu.CompilerParams(
            collective_id=0, has_side_effects=True, vmem_limit_bytes=60 * 2**20
        ),
    )(
        qkv,
        residual,
        text,
        bias,
        attn_gate,
        w_out,
        final_mod,
        w_final,
        noisy.reshape(ROWS, 64),
        conv_weight.reshape(48, 512),
        conv_bias.reshape(1, 512),
    )
    return velocity.reshape(2, 64, 64), decoded.reshape(2, 64, 2, 512)


def solution(mesh):
    return jax.shard_map(
        shards,
        mesh=mesh,
        in_specs=(
            P("cfg", "blk", "sp", None),
            P("cfg", "blk", "sp", None),
            P("cfg", None, None, None, None),
            P("cfg"),
            P("cfg", None),
            P("cfg", None),
            P(),
            P("cfg", None, None),
            P(),
            P("blk", "sp", None),
            P(),
            P(),
        ),
        out_specs=(P("blk", "sp", None), P("blk", "sp", "cfg", None)),
        check_vma=False,
    )
```

```python
import functools
import math

import jax
import jax.numpy as jnp
from jax import lax
from jax.experimental import pallas as pl
from jax.experimental.pallas import tpu as pltpu
from jax.sharding import PartitionSpec as P

D = 3072
H = 24
HD = 128
G = 3
TXT = 256
ROWS = 128
QB = 256
MESH = pl.DeviceIdType.MESH
SCALE = math.log2(math.e) / math.sqrt(HD)
BF = jnp.bfloat16
F32 = jnp.float32

guidance_scale = 6.0
sigma_last = 0.125
vae_factor = 0.476986
norm_eps = 1e-06


def wait_bytes(ref, sem):
    pltpu.make_async_copy(ref, ref, sem).wait()


def body(
    qkv, residual, text, tlen, keep, gate, w_out, fmod, w_fin, noisy,
    guided_out, latents,
    qb, kv, ob, att, po, pr, so, sr, tb, mo, mb, wo, res, wf, proj, mod, pb, lat, halo, acc, m_s, l_s,
    snd, rcv_q, rcv_k, rcv_v, ysnd, yrcv, dsnd, drcv, psnd, prcv, osnd, orcv, lsem, tsnd, trcv, gsnd, grcv, hsnd, hrcv,
):
    c = lax.axis_index("cfg")
    b = lax.axis_index("blk")
    s = lax.axis_index("sp")
    xl = b // 4
    y = b % 4
    to_q = (c, xl * 4 + y + 1 - 2 * (y % 2), s)
    to_k = (c, xl * 4 + 3 - y, s)
    to_core = (1 - c, b, s)
    moved = c != xl

    def peer(d):
        return (xl, c * 4 + y, d)

    def remote(src, dst, send, recv, dev):
        return pltpu.make_async_remote_copy(src, dst, send, recv, device_id=dev, device_id_type=MESH)

    fetch_w = pltpu.make_async_copy(w_out, wo, lsem.at[0])
    fetch_r = pltpu.make_async_copy(residual.at[0], res, lsem.at[1])
    fetch_f = pltpu.make_async_copy(w_fin, wf, lsem.at[2])

    bar = pltpu.get_barrier_semaphore()

    def sig(dev):
        pl.semaphore_signal(bar, inc=1, device_id=dev, device_id_type=MESH)

    sig(to_q)
    sig(to_k)
    sig(to_core)
    for j in range(1, 8):
        sig(peer((s + j) % 8))

    @pl.when(moved)
    def _():
        sig(peer(s))

    @pl.when(b < 7)
    def _():
        sig((c, b + 1, s))

    @pl.when(b > 0)
    def _():
        sig((c, b - 1, s))

    kept = (lax.broadcasted_iota(jnp.int32, (1, TXT), 1) < tlen[0]) & (keep[...] == 1)
    mo[...] = jnp.broadcast_to(jnp.where(kept, 0.0, -1e30).astype(F32), (8, TXT))

    count = 10 + jnp.where(moved, 1, 0) + jnp.where(b < 7, 1, 0) + jnp.where(b > 0, 1, 0)
    pl.semaphore_wait(bar, count)

    rcvs = (rcv_q, rcv_k, rcv_v)

    def send_head(h):
        for kind in (1, 2, 0):
            landing = qb.at[h, 0, s] if kind == 0 else kv.at[h, 0, xl, kind - 1, s]

            def piece(d):
                return qkv.at[0, :, :, pl.ds(pl.multiple_of(kind * D + (d * G + h) * HD, HD), HD)]

            def one(j, carry):
                d = (s + j) % 8
                remote(piece(d), landing, snd.at[h, kind], rcvs[kind].at[h], peer(d)).start()
                return carry

            lax.fori_loop(1, 8, one, 0)

            @pl.when(moved)
            def _():
                remote(piece(s), landing, snd.at[h, kind], rcvs[kind].at[h], peer(s)).start()

            @pl.when(jnp.logical_not(moved))
            def _():
                pltpu.make_async_copy(piece(s), landing, rcvs[kind].at[h]).start()

    def share_head(h):
        for kind in range(2):
            wait_bytes(kv.at[h, 0, c, kind], (rcv_k, rcv_v)[kind].at[h])
            mine = kv.at[h, 0, c, kind]
            remote(mine, kv.at[h, 1, c, kind], ysnd.at[h, kind], yrcv.at[h, kind], to_k).start()
            remote(mine, mine, dsnd.at[h, 0, kind], drcv.at[h, 0, kind], to_core).start()
        wait_bytes(qb.at[h, 0], rcv_q.at[h])
        remote(qb.at[h, 0], qb.at[h, 1], ysnd.at[h, 2], yrcv.at[h, 2], to_q).start()

    def pass_far(h):
        for kind in range(2):
            far = kv.at[h, 1, c, kind]
            wait_bytes(far, yrcv.at[h, kind])
            remote(far, far, dsnd.at[h, 1, kind], drcv.at[h, 1, kind], to_core).start()

    def wait_core(h, far):
        for kind in range(2):
            wait_bytes(kv.at[h, far, 1 - c, kind], drcv.at[h, far, kind])

    text_own = pltpu.make_async_copy(text, tb.at[c], lsem.at[3])
    text_out = remote(text, tb.at[c], tsnd.at[0], trcv.at[0], to_core)
    mask_own = pltpu.make_async_copy(mo, mb.at[c], lsem.at[4])
    mask_out = remote(mo, mb.at[c], tsnd.at[1], trcv.at[1], to_core)

    send_head(0)
    text_own.start()
    text_out.start()
    mask_own.start()
    mask_out.start()
    send_head(1)
    send_head(2)
    fetch_w.start()
    fetch_r.start()
    fetch_f.start()

    text_own.wait()
    mask_own.wait()
    wait_bytes(tb.at[1 - c], trcv.at[0])
    wait_bytes(mb.at[1 - c], trcv.at[1])

    def queries(h, r, u):
        return qb[h, r, pl.ds(2 * u, 2)].reshape(QB, HD)

    def scores(q, keys):
        return lax.dot_general(q, keys, (((1,), (1,)), ((), ())), preferred_element_type=F32)

    def weigh(weights, values):
        padded = jnp.concatenate([values, jnp.ones_like(values)], axis=1)
        return jnp.dot(weights.astype(BF), padded, preferred_element_type=F32)

    blocks = 1024 // QB

    def text_step(h):
        keys = tb[xl, h, 0]
        values = tb[xl, h, 1]
        added = mb[xl]
        par = h % 2
        for u in range(blocks):
            rows = pl.ds(u * QB, QB)
            sc = scores(queries(h, 0, u), keys) + added[0:1]
            top = jnp.max(sc, axis=1, keepdims=True)
            out = weigh(jnp.exp2((sc - top) * SCALE), values)
            m_s[par, 0, rows] = jnp.broadcast_to(top, (QB, HD))
            acc[par, 0, rows] = out[:, :HD]
            l_s[par, 0, rows] = out[:, HD:]

    def softmax_blocks(h, far, rowsets, done):
        keys = kv[h, far, :, 0].reshape(2048, HD)
        values = kv[h, far, :, 1].reshape(2048, HD)
        par = h % 2
        order = [(r, u) for r in rowsets for u in range(blocks)]
        now = scores(queries(h, *order[0]), keys)
        for i, (r, u) in enumerate(order):
            later = scores(queries(h, *order[i + 1]), keys) if i + 1 < len(order) else None
            rows = pl.ds(u * QB, QB)
            top = jnp.max(now, axis=1, keepdims=True)
            if far == 0 and r == 1:
                new = jnp.broadcast_to(top, (QB, HD))
                out = weigh(jnp.exp2((now - top) * SCALE), values)
                total, weight = out[:, :HD], out[:, HD:]
            else:
                old = m_s[par, r, rows]
                new = jnp.maximum(old, top)
                factor = jnp.exp2((old - new) * SCALE)
                out = weigh(jnp.exp2((now - new[:, :1]) * SCALE), values)
                total = acc[par, r, rows] * factor + out[:, :HD]
                weight = l_s[par, r, rows] * factor + out[:, HD:]
            if r == 1 and far == 1:
                done(u, new, total, weight)
            else:
                m_s[par, r, rows] = new
                acc[par, r, rows] = total
                l_s[par, r, rows] = weight
            now = later

    def far_step(h):
        def done(u, top, total, weight):
            cols = pl.ds(u * QB, QB)
            po[h, pl.ds(2 * u, 2)] = (total / weight).astype(BF).reshape(2, 2, 64, HD)
            lane = lax.broadcasted_iota(jnp.int32, (QB, HD), 1)
            so[h, :, cols] = jnp.where(lane == 0, top, weight).T[0:8]
            part = po.at[h, pl.ds(2 * u, 2)]
            remote(part, pr.at[h, pl.ds(2 * u, 2)], psnd.at[h, 0], prcv.at[h, 0], to_q).start()
            remote(so.at[h, :, cols], sr.at[h, :, cols], psnd.at[h, 1], prcv.at[h, 1], to_q).start()

        softmax_blocks(h, 1, (1, 0), done)

    def join(h):
        wait_bytes(pr.at[h], prcv.at[h, 0])
        wait_bytes(sr.at[h], prcv.at[h, 1])
        par = h % 2

        def block(j, carry):
            u = (j + s // 2) % blocks
            rows = pl.ds(pl.multiple_of(u * QB, QB), QB)
            stats = sr[h, :, rows].T
            top_p = stats[:, 0:1]
            sum_p = stats[:, 1:2]
            top_a = m_s[par, 0, rows]
            new = jnp.maximum(top_a, top_p)
            f_a = jnp.exp2((top_a - new) * SCALE)
            f_p = jnp.exp2((top_p - new) * SCALE) * sum_p
            partial = pr[h, pl.ds(2 * u, 2)].reshape(QB, HD).astype(F32)
            out = (acc[par, 0, rows] * f_a + partial * f_p) / (l_s[par, 0, rows] * f_a + f_p)
            ob[h, pl.ds(2 * u, 2)] = out.astype(BF).reshape(2, 2, 64, HD)
            for k in range(2):
                d = 2 * u + k

                @pl.when(jnp.logical_or(moved, d != s))
                def _():
                    remote(ob.at[h, d], att.at[s, h], osnd.at[h], orcv.at[h], peer(d)).start()

                @pl.when(jnp.logical_not(jnp.logical_or(moved, d != s)))
                def _():
                    pltpu.make_async_copy(ob.at[h, d], att.at[s, h], orcv.at[h]).start()

            return carry

        lax.fori_loop(0, blocks, block, 0)

    def project(h):
        wait_bytes(att.at[:, h], orcv.at[h])
        rows = jnp.concatenate([att[d, h].reshape(ROWS, HD) for d in range(8)], axis=1)

        def columns(n, carry):
            cols = pl.ds(pl.multiple_of(n * 512, 512), 512)
            weight = jnp.concatenate(
                [wo[pl.ds(pl.multiple_of((d * G + h) * HD, HD), HD), cols] for d in range(8)], axis=0
            )
            proj[:, cols] += jnp.dot(rows, weight, preferred_element_type=F32)
            return carry

        lax.fori_loop(0, D // 512, columns, 0)

    proj[...] = jnp.zeros_like(proj)
    share_head(0)
    wait_core(0, 0)
    text_step(0)
    softmax_blocks(0, 0, (0,), None)
    wait_bytes(qb.at[0, 1], yrcv.at[0, 2])
    softmax_blocks(0, 0, (1,), None)

    def step(h, carry):
        @pl.when(h < 2)
        def _():
            share_head(h + 1)

        pass_far(h)

        @pl.when(h < 2)
        def _():
            wait_core(h + 1, 0)
            text_step(h + 1)
            softmax_blocks(h + 1, 0, (0,), None)

        @pl.when(h == 1)
        def _():
            fetch_w.wait()

        @pl.when(h > 0)
        def _():
            project(h - 1)

        wait_core(h, 1)
        far_step(h)

        @pl.when(h < 2)
        def _():
            wait_bytes(qb.at[h + 1, 1], yrcv.at[h + 1, 2])
            softmax_blocks(h + 1, 0, (1,), None)

        join(h)
        return carry

    lax.fori_loop(0, G, step, 0)
    project(G - 1)

    fetch_r.wait()
    fetch_f.wait()

    def norm(n, carry):
        rows = pl.ds(pl.multiple_of(n * 32, 32), 32)
        shown = res[n // 2, pl.ds(pl.multiple_of((n % 2) * 32, 32), 32)].astype(F32)
        hidden = shown + gate[...] * proj[rows]
        centered = hidden - jnp.mean(hidden, axis=1, keepdims=True)
        normed = centered * lax.rsqrt(jnp.mean(centered * centered, axis=1, keepdims=True) + norm_eps)
        mod[rows] = (normed * (1.0 + fmod[0, 1:2]) + fmod[0, 0:1]).astype(BF)
        return carry

    lax.fori_loop(0, 4, norm, 0)
    pb[c] = lax.dot_general(mod[...], wf[...], (((1,), (1,)), ((), ())), preferred_element_type=F32)
    remote(pb.at[c], pb.at[c], gsnd, grcv, to_core).start()
    wait_bytes(pb.at[1 - c], grcv)
    uncond = pb[1]
    guided = uncond + guidance_scale * (pb[0] - uncond)
    guided_out[...] = guided
    lat[...] = ((noisy[...] - sigma_last * guided) / vae_factor).astype(BF)

    @pl.when(b < 7)
    def _():
        remote(lat, halo, hsnd, hrcv, (c, b + 1, s)).start()

    latents[1] = lat[...]

    @pl.when(b == 0)
    def _():
        latents[0] = jnp.zeros_like(halo)

    @pl.when(b > 0)
    def _():
        wait_bytes(halo, hrcv)
        latents[0] = halo[...]

    for h in range(G):
        for kind in range(3):
            wait_bytes(qb.at[h, 0, pl.ds(0, 7)], snd.at[h, kind])

            @pl.when(moved)
            def _():
                wait_bytes(qb.at[h, 0, 0], snd.at[h, kind])

            wait_bytes(kv.at[h, 0, c, 0], ysnd.at[h, kind])
        for far in range(2):
            for kind in range(2):
                wait_bytes(kv.at[h, 0, c, 0], dsnd.at[h, far, kind])
        wait_bytes(po.at[h], psnd.at[h, 0])
        wait_bytes(so.at[h], psnd.at[h, 1])
        wait_bytes(ob.at[h, pl.ds(0, 7)], osnd.at[h])

        @pl.when(moved)
        def _():
            wait_bytes(ob.at[h, 0], osnd.at[h])

    wait_bytes(tb.at[c], tsnd.at[0])
    wait_bytes(mb.at[c], tsnd.at[1])
    wait_bytes(pb.at[c], gsnd)

    @pl.when(b < 7)
    def _():
        wait_bytes(lat, hsnd)


def conv_body(guided, latents, conv_w, conv_b, velocity, decoded):
    c = lax.axis_index("cfg")
    velocity[...] = guided[...].reshape(2, 64, 64)
    before = latents[0]
    here = latents[1]
    across = jnp.concatenate([before[64:], here[:64]], axis=0)
    entry = lax.broadcasted_iota(jnp.int32, (64, 48), 0)
    place = lax.broadcasted_iota(jnp.int32, (64, 48), 1)
    outs = []
    for i in range(2):
        taps = jnp.zeros((ROWS, 48), F32)
        for t, frames in enumerate((before, across, here)):
            chosen = (entry == 4 * (place - 16 * t) + 2 * c + i) & (place >= 16 * t) & (place < 16 * t + 16)
            taps = taps + jnp.dot(frames, jnp.where(chosen, 1.0, 0.0).astype(BF), preferred_element_type=F32)
        out = jnp.dot(taps.astype(BF), conv_w[...], preferred_element_type=F32) + conv_b[...]
        outs.append(out.reshape(2, 64, 512))
    decoded[...] = jnp.stack(outs, axis=2).astype(BF)


def shards(qkv, residual, text_kv, text_len, text_keep, attn_gate, w_out, final_mod, w_final, noisy, conv_weight, conv_bias):
    text = lax.dynamic_slice_in_dim(text_kv[0], lax.axis_index("sp") * G, G, axis=2)
    text = jnp.transpose(text, (2, 1, 0, 3))
    hbm = pl.BlockSpec(memory_space=pl.ANY)
    vmem = pl.BlockSpec(memory_space=pltpu.VMEM)
    smem = pl.BlockSpec(memory_space=pltpu.SMEM)
    dma = pltpu.SemaphoreType.DMA
    guided, latents = pl.pallas_call(
        body,
        out_shape=(
            jax.ShapeDtypeStruct((ROWS, 64), F32),
            jax.ShapeDtypeStruct((2, ROWS, 64), BF),
        ),
        in_specs=[hbm, hbm, vmem, smem, vmem, vmem, hbm, vmem, hbm, vmem],
        out_specs=(vmem, vmem),
        scratch_shapes=[
            pltpu.VMEM((G, 2, 8, 2, 64, HD), BF),
            pltpu.VMEM((G, 2, 2, 2, 8, 2, 64, HD), BF),
            pltpu.VMEM((G, 8, 2, 64, HD), BF),
            pltpu.VMEM((8, G, 2, 64, HD), BF),
            pltpu.VMEM((G, 8, 2, 64, HD), BF),
            pltpu.VMEM((G, 8, 2, 64, HD), BF),
            pltpu.VMEM((G, 8, 1024), F32),
            pltpu.VMEM((G, 8, 1024), F32),
            pltpu.VMEM((2, G, 2, TXT, HD), BF),
            pltpu.VMEM((8, TXT), F32),
            pltpu.VMEM((2, 8, TXT), F32),
            pltpu.VMEM((D, D), BF),
            pltpu.VMEM((2, 64, D), BF),
            pltpu.VMEM((64, D), BF),
            pltpu.VMEM((ROWS, D), F32),
            pltpu.VMEM((ROWS, D), BF),
            pltpu.VMEM((2, ROWS, 64), F32),
            pltpu.VMEM((ROWS, 64), BF),
            pltpu.VMEM((ROWS, 64), BF),
            pltpu.VMEM((2, 2, 1024, HD), F32),
            pltpu.VMEM((2, 2, 1024, HD), F32),
            pltpu.VMEM((2, 2, 1024, HD), F32),
            dma((G, 3)),
            dma((G,)),
            dma((G,)),
            dma((G,)),
            dma((G, 3)),
            dma((G, 3)),
            dma((G, 2, 2)),
            dma((G, 2, 2)),
            dma((G, 2)),
            dma((G, 2)),
            dma((G,)),
            dma((G,)),
            dma((5,)),
            dma((2,)),
            dma((2,)),
            dma,
            dma,
            dma,
            dma,
        ],
        compiler_params=pltpu.CompilerParams(
            collective_id=0, has_side_effects=True, vmem_limit_bytes=60 * 2**20
        ),
    )(
        qkv,
        residual,
        text,
        text_len,
        text_keep,
        attn_gate,
        w_out,
        final_mod,
        w_final.T,
        noisy.reshape(ROWS, 64),
    )
    return pl.pallas_call(
        conv_body,
        out_shape=(
            jax.ShapeDtypeStruct((2, 64, 64), F32),
            jax.ShapeDtypeStruct((2, 64, 2, 512), BF),
        ),
        in_specs=[vmem] * 4,
        out_specs=(vmem, vmem),
    )(guided, latents, conv_weight.reshape(48, 512), conv_bias.reshape(1, 512))


def solution(mesh):
    return jax.shard_map(
        shards,
        mesh=mesh,
        in_specs=(
            P("cfg", "blk", "sp", None),
            P("cfg", "blk", "sp", None),
            P("cfg", None, None, None, None),
            P("cfg"),
            P("cfg", None),
            P("cfg", None),
            P(),
            P("cfg", None, None),
            P(),
            P("blk", "sp", None),
            P(),
            P(),
        ),
        out_specs=(P("blk", "sp", None), P("blk", "sp", "cfg", None)),
        check_vma=False,
    )
```

```python
import functools
import math

import jax
import jax.numpy as jnp
from jax import lax
from jax.experimental import pallas as pl
from jax.experimental.pallas import tpu as pltpu
from jax.sharding import PartitionSpec as P

D = 3072
H = 24
HD = 128
G = 3
TXT = 256
ROWS = 128
QB = 256
MESH = pl.DeviceIdType.MESH
SCALE = math.log2(math.e) / math.sqrt(HD)
BF = jnp.bfloat16
F32 = jnp.float32

guidance_scale = 6.0
sigma_last = 0.125
vae_factor = 0.476986
norm_eps = 1e-06


def wait_bytes(ref, sem):
    pltpu.make_async_copy(ref, ref, sem).wait()


def body(
    qkv, residual, text, tlen, keep, gate, w_out, fmod, w_fin, noisy,
    guided_out, latents,
    qb, kv, ob, att, po, pr, so, sr, tb, mo, mb, wo, res, wf, proj, mod, pb, lat, halo, acc, m_s, l_s,
    snd, rcv_q, rcv_k, rcv_v, ysnd, yrcv, dsnd, drcv, psnd, prcv, osnd, orcv, lsem, tsnd, trcv, gsnd, grcv, hsnd, hrcv,
):
    c = lax.axis_index("cfg")
    b = lax.axis_index("blk")
    s = lax.axis_index("sp")
    xl = b // 4
    y = b % 4
    to_q = (c, xl * 4 + y + 1 - 2 * (y % 2), s)
    to_k = (c, xl * 4 + 3 - y, s)
    to_core = (1 - c, b, s)
    moved = c != xl

    def peer(d):
        return (xl, c * 4 + y, d)

    def remote(src, dst, send, recv, dev):
        return pltpu.make_async_remote_copy(src, dst, send, recv, device_id=dev, device_id_type=MESH)

    fetch_w = pltpu.make_async_copy(w_out, wo, lsem.at[0])
    fetch_r = pltpu.make_async_copy(residual.at[0], res, lsem.at[1])
    fetch_f = pltpu.make_async_copy(w_fin, wf, lsem.at[2])

    bar = pltpu.get_barrier_semaphore()

    def sig(dev):
        pl.semaphore_signal(bar, inc=1, device_id=dev, device_id_type=MESH)

    sig(to_q)
    sig(to_k)
    sig(to_core)
    for j in range(1, 8):
        sig(peer((s + j) % 8))

    @pl.when(moved)
    def _():
        sig(peer(s))

    @pl.when(b < 7)
    def _():
        sig((c, b + 1, s))

    @pl.when(b > 0)
    def _():
        sig((c, b - 1, s))

    kept = (lax.broadcasted_iota(jnp.int32, (1, TXT), 1) < tlen[0]) & (keep[...] == 1)
    mo[...] = jnp.broadcast_to(jnp.where(kept, 0.0, -1e30).astype(F32), (8, TXT))

    count = 10 + jnp.where(moved, 1, 0) + jnp.where(b < 7, 1, 0) + jnp.where(b > 0, 1, 0)
    pl.semaphore_wait(bar, count)

    rcvs = (rcv_q, rcv_k, rcv_v)

    def send_head(h):
        for kind in (1, 2, 0):
            landing = qb.at[h, 0, s] if kind == 0 else kv.at[h, 0, xl, kind - 1, s]

            def piece(d):
                return qkv.at[0, :, :, pl.ds(pl.multiple_of(kind * D + (d * G + h) * HD, HD), HD)]

            def one(j, carry):
                d = (s + j) % 8
                remote(piece(d), landing, snd.at[h, kind], rcvs[kind].at[h], peer(d)).start()
                return carry

            lax.fori_loop(1, 8, one, 0)

            @pl.when(moved)
            def _():
                remote(piece(s), landing, snd.at[h, kind], rcvs[kind].at[h], peer(s)).start()

            @pl.when(jnp.logical_not(moved))
            def _():
                pltpu.make_async_copy(piece(s), landing, rcvs[kind].at[h]).start()

    def share_keys(h):
        for kind in range(2):
            wait_bytes(kv.at[h, 0, c, kind], (rcv_k, rcv_v)[kind].at[h])
            mine = kv.at[h, 0, c, kind]
            remote(mine, kv.at[h, 1, c, kind], ysnd.at[h, kind], yrcv.at[h, kind], to_k).start()
            remote(mine, mine, dsnd.at[h, 0, kind], drcv.at[h, 0, kind], to_core).start()

    def share_queries(h):
        wait_bytes(qb.at[h, 0], rcv_q.at[h])
        remote(qb.at[h, 0], qb.at[h, 1], ysnd.at[h, 2], yrcv.at[h, 2], to_q).start()

    def pass_far(h):
        for kind in range(2):
            far = kv.at[h, 1, c, kind]
            wait_bytes(far, yrcv.at[h, kind])
            remote(far, far, dsnd.at[h, 1, kind], drcv.at[h, 1, kind], to_core).start()

    def wait_core(h, far):
        for kind in range(2):
            wait_bytes(kv.at[h, far, 1 - c, kind], drcv.at[h, far, kind])

    text_own = pltpu.make_async_copy(text, tb.at[c], lsem.at[3])
    text_out = remote(text, tb.at[c], tsnd.at[0], trcv.at[0], to_core)
    mask_own = pltpu.make_async_copy(mo, mb.at[c], lsem.at[4])
    mask_out = remote(mo, mb.at[c], tsnd.at[1], trcv.at[1], to_core)

    send_head(0)
    text_own.start()
    text_out.start()
    mask_own.start()
    mask_out.start()
    send_head(1)
    send_head(2)
    fetch_w.start()
    fetch_r.start()
    fetch_f.start()

    def queries(h, r, u):
        return qb[h, r, pl.ds(2 * u, 2)].reshape(QB, HD)

    def scores(q, keys):
        return lax.dot_general(q, keys, (((1,), (1,)), ((), ())), preferred_element_type=F32)

    def weigh(weights, values):
        padded = jnp.concatenate([values, jnp.ones_like(values)], axis=1)
        return jnp.dot(weights.astype(BF), padded, preferred_element_type=F32)

    blocks = 1024 // QB

    def softmax_blocks(h, far, rowsets, done=None):
        keys = kv[h, far, :, 0].reshape(2048, HD)
        values = kv[h, far, :, 1].reshape(2048, HD)
        with_text = far == 0 and rowsets == (0,)
        if with_text:
            text_keys = tb[xl, h, 0]
            text_values = tb[xl, h, 1]
            added = mb[xl]
        par = h % 2
        order = [(r, u) for r in rowsets for u in range(blocks)]

        def all_scores(r, u):
            q = queries(h, r, u)
            if not with_text:
                return scores(q, keys), None
            return scores(q, keys), scores(q, text_keys) + added[0:1]

        ahead = all_scores(*order[0])
        for i, (r, u) in enumerate(order):
            now, now_text = ahead
            if i + 1 < len(order):
                ahead = all_scores(*order[i + 1])
            rows = pl.ds(u * QB, QB)
            top = jnp.max(now, axis=1, keepdims=True)
            if far == 0:
                if with_text:
                    top = jnp.maximum(top, jnp.max(now_text, axis=1, keepdims=True))
                new = jnp.broadcast_to(top, (QB, HD))
                out = weigh(jnp.exp2((now - top) * SCALE), values)
                if with_text:
                    out = out + weigh(jnp.exp2((now_text - top) * SCALE), text_values)
                total, weight = out[:, :HD], out[:, HD:]
            else:
                old = m_s[par, r, rows]
                new = jnp.maximum(old, top)
                factor = jnp.exp2((old - new) * SCALE)
                out = weigh(jnp.exp2((now - new[:, :1]) * SCALE), values)
                total = acc[par, r, rows] * factor + out[:, :HD]
                weight = l_s[par, r, rows] * factor + out[:, HD:]
            if r == 1 and far == 1:
                done(u, new, total, weight)
            else:
                m_s[par, r, rows] = new
                acc[par, r, rows] = total
                l_s[par, r, rows] = weight

    def far_step(h):
        def done(u, top, total, weight):
            cols = pl.ds(u * QB, QB)
            po[h, pl.ds(2 * u, 2)] = (total / weight).astype(BF).reshape(2, 2, 64, HD)
            lane = lax.broadcasted_iota(jnp.int32, (QB, HD), 1)
            so[h, :, cols] = jnp.where(lane == 0, top, weight).T[0:8]
            part = po.at[h, pl.ds(2 * u, 2)]
            remote(part, pr.at[h, pl.ds(2 * u, 2)], psnd.at[h, 0], prcv.at[h, 0], to_q).start()
            remote(so.at[h, :, cols], sr.at[h, :, cols], psnd.at[h, 1], prcv.at[h, 1], to_q).start()

        softmax_blocks(h, 1, (1, 0), done)

    def join(h):
        wait_bytes(pr.at[h], prcv.at[h, 0])
        wait_bytes(sr.at[h], prcv.at[h, 1])
        par = h % 2

        def block(j, carry):
            u = (j + s // 2) % blocks
            rows = pl.ds(pl.multiple_of(u * QB, QB), QB)
            stats = sr[h, :, rows].T
            top_p = stats[:, 0:1]
            sum_p = stats[:, 1:2]
            top_a = m_s[par, 0, rows]
            new = jnp.maximum(top_a, top_p)
            f_a = jnp.exp2((top_a - new) * SCALE)
            f_p = jnp.exp2((top_p - new) * SCALE) * sum_p
            partial = pr[h, pl.ds(2 * u, 2)].reshape(QB, HD).astype(F32)
            out = (acc[par, 0, rows] * f_a + partial * f_p) / (l_s[par, 0, rows] * f_a + f_p)
            ob[h, pl.ds(2 * u, 2)] = out.astype(BF).reshape(2, 2, 64, HD)
            for k in range(2):
                d = 2 * u + k

                @pl.when(jnp.logical_or(moved, d != s))
                def _():
                    remote(ob.at[h, d], att.at[s, h], osnd.at[h], orcv.at[h], peer(d)).start()

                @pl.when(jnp.logical_not(jnp.logical_or(moved, d != s)))
                def _():
                    pltpu.make_async_copy(ob.at[h, d], att.at[s, h], orcv.at[h]).start()

            return carry

        lax.fori_loop(0, blocks, block, 0)

    def project(h):
        wait_bytes(att.at[:, h], orcv.at[h])
        rows = jnp.concatenate([att[d, h].reshape(ROWS, HD) for d in range(8)], axis=1)

        def columns(n, carry):
            cols = pl.ds(pl.multiple_of(n * 512, 512), 512)
            weight = jnp.concatenate(
                [wo[pl.ds(pl.multiple_of((d * G + h) * HD, HD), HD), cols] for d in range(8)], axis=0
            )
            proj[:, cols] += jnp.dot(rows, weight, preferred_element_type=F32)
            return carry

        lax.fori_loop(0, D // 512, columns, 0)

    def own_step(h):
        wait_core(h, 0)
        softmax_blocks(h, 0, (0,))

    def shared_step(h):
        wait_bytes(qb.at[h, 1], yrcv.at[h, 2])
        softmax_blocks(h, 0, (1,))

    share_keys(0)
    share_queries(0)
    proj[...] = jnp.zeros_like(proj)
    text_own.wait()
    mask_own.wait()
    wait_bytes(tb.at[1 - c], trcv.at[0])
    wait_bytes(mb.at[1 - c], trcv.at[1])
    own_step(0)
    share_keys(1)
    pass_far(0)
    shared_step(0)

    def step(h, carry):
        @pl.when(h < 2)
        def _():
            share_queries(h + 1)
            own_step(h + 1)

        @pl.when(h == 2)
        def _():
            fetch_w.wait()
            project(0)

        wait_core(h, 1)
        far_step(h)

        @pl.when(h == 0)
        def _():
            share_keys(2)

        @pl.when(h < 2)
        def _():
            pass_far(h + 1)
            shared_step(h + 1)

        @pl.when(h == 2)
        def _():
            project(1)

        join(h)
        return carry

    lax.fori_loop(0, G, step, 0)
    project(G - 1)

    fetch_r.wait()
    fetch_f.wait()

    def norm(n, carry):
        rows = pl.ds(pl.multiple_of(n * 32, 32), 32)
        shown = res[n // 2, pl.ds(pl.multiple_of((n % 2) * 32, 32), 32)].astype(F32)
        hidden = shown + gate[...] * proj[rows]
        centered = hidden - jnp.mean(hidden, axis=1, keepdims=True)
        normed = centered * lax.rsqrt(jnp.mean(centered * centered, axis=1, keepdims=True) + norm_eps)
        mod[rows] = (normed * (1.0 + fmod[0, 1:2]) + fmod[0, 0:1]).astype(BF)
        return carry

    lax.fori_loop(0, 4, norm, 0)
    pb[c] = lax.dot_general(mod[...], wf[...], (((1,), (1,)), ((), ())), preferred_element_type=F32)
    remote(pb.at[c], pb.at[c], gsnd, grcv, to_core).start()
    wait_bytes(pb.at[1 - c], grcv)
    uncond = pb[1]
    guided = uncond + guidance_scale * (pb[0] - uncond)
    guided_out[...] = guided
    lat[...] = ((noisy[...] - sigma_last * guided) / vae_factor).astype(BF)

    @pl.when(b < 7)
    def _():
        remote(lat, halo, hsnd, hrcv, (c, b + 1, s)).start()

    latents[1] = lat[...]

    @pl.when(b == 0)
    def _():
        latents[0] = jnp.zeros_like(halo)

    @pl.when(b > 0)
    def _():
        wait_bytes(halo, hrcv)
        latents[0] = halo[...]

    for h in range(G):
        for kind in range(3):
            wait_bytes(qb.at[h, 0, pl.ds(0, 7)], snd.at[h, kind])

            @pl.when(moved)
            def _():
                wait_bytes(qb.at[h, 0, 0], snd.at[h, kind])

            wait_bytes(kv.at[h, 0, c, 0], ysnd.at[h, kind])
        for far in range(2):
            for kind in range(2):
                wait_bytes(kv.at[h, 0, c, 0], dsnd.at[h, far, kind])
        wait_bytes(po.at[h], psnd.at[h, 0])
        wait_bytes(so.at[h], psnd.at[h, 1])
        wait_bytes(ob.at[h, pl.ds(0, 7)], osnd.at[h])

        @pl.when(moved)
        def _():
            wait_bytes(ob.at[h, 0], osnd.at[h])

    wait_bytes(tb.at[c], tsnd.at[0])
    wait_bytes(mb.at[c], tsnd.at[1])
    wait_bytes(pb.at[c], gsnd)

    @pl.when(b < 7)
    def _():
        wait_bytes(lat, hsnd)


def conv_body(guided, latents, conv_w, conv_b, velocity, decoded):
    c = lax.axis_index("cfg")
    velocity[...] = guided[...].reshape(2, 64, 64)
    before = latents[0]
    here = latents[1]
    across = jnp.concatenate([before[64:], here[:64]], axis=0)
    entry = lax.broadcasted_iota(jnp.int32, (64, 48), 0)
    place = lax.broadcasted_iota(jnp.int32, (64, 48), 1)
    outs = []
    for i in range(2):
        taps = jnp.zeros((ROWS, 48), F32)
        for t, frames in enumerate((before, across, here)):
            chosen = (entry == 4 * (place - 16 * t) + 2 * c + i) & (place >= 16 * t) & (place < 16 * t + 16)
            taps = taps + jnp.dot(frames, jnp.where(chosen, 1.0, 0.0).astype(BF), preferred_element_type=F32)
        out = jnp.dot(taps.astype(BF), conv_w[...], preferred_element_type=F32) + conv_b[...]
        outs.append(out.reshape(2, 64, 512))
    decoded[...] = jnp.stack(outs, axis=2).astype(BF)


def shards(qkv, residual, text_kv, text_len, text_keep, attn_gate, w_out, final_mod, w_final, noisy, conv_weight, conv_bias):
    text = lax.dynamic_slice_in_dim(text_kv[0], lax.axis_index("sp") * G, G, axis=2)
    text = jnp.transpose(text, (2, 1, 0, 3))
    hbm = pl.BlockSpec(memory_space=pl.ANY)
    vmem = pl.BlockSpec(memory_space=pltpu.VMEM)
    smem = pl.BlockSpec(memory_space=pltpu.SMEM)
    dma = pltpu.SemaphoreType.DMA
    guided, latents = pl.pallas_call(
        body,
        out_shape=(
            jax.ShapeDtypeStruct((ROWS, 64), F32),
            jax.ShapeDtypeStruct((2, ROWS, 64), BF),
        ),
        in_specs=[hbm, hbm, vmem, smem, vmem, vmem, hbm, vmem, hbm, vmem],
        out_specs=(vmem, vmem),
        scratch_shapes=[
            pltpu.VMEM((G, 2, 8, 2, 64, HD), BF),
            pltpu.VMEM((G, 2, 2, 2, 8, 2, 64, HD), BF),
            pltpu.VMEM((G, 8, 2, 64, HD), BF),
            pltpu.VMEM((8, G, 2, 64, HD), BF),
            pltpu.VMEM((G, 8, 2, 64, HD), BF),
            pltpu.VMEM((G, 8, 2, 64, HD), BF),
            pltpu.VMEM((G, 8, 1024), F32),
            pltpu.VMEM((G, 8, 1024), F32),
            pltpu.VMEM((2, G, 2, TXT, HD), BF),
            pltpu.VMEM((8, TXT), F32),
            pltpu.VMEM((2, 8, TXT), F32),
            pltpu.VMEM((D, D), BF),
            pltpu.VMEM((2, 64, D), BF),
            pltpu.VMEM((64, D), BF),
            pltpu.VMEM((ROWS, D), F32),
            pltpu.VMEM((ROWS, D), BF),
            pltpu.VMEM((2, ROWS, 64), F32),
            pltpu.VMEM((ROWS, 64), BF),
            pltpu.VMEM((ROWS, 64), BF),
            pltpu.VMEM((2, 2, 1024, HD), F32),
            pltpu.VMEM((2, 2, 1024, HD), F32),
            pltpu.VMEM((2, 2, 1024, HD), F32),
            dma((G, 3)),
            dma((G,)),
            dma((G,)),
            dma((G,)),
            dma((G, 3)),
            dma((G, 3)),
            dma((G, 2, 2)),
            dma((G, 2, 2)),
            dma((G, 2)),
            dma((G, 2)),
            dma((G,)),
            dma((G,)),
            dma((5,)),
            dma((2,)),
            dma((2,)),
            dma,
            dma,
            dma,
            dma,
        ],
        compiler_params=pltpu.CompilerParams(
            collective_id=0, has_side_effects=True, vmem_limit_bytes=60 * 2**20
        ),
    )(
        qkv,
        residual,
        text,
        text_len,
        text_keep,
        attn_gate,
        w_out,
        final_mod,
        w_final.T,
        noisy.reshape(ROWS, 64),
    )
    return pl.pallas_call(
        conv_body,
        out_shape=(
            jax.ShapeDtypeStruct((2, 64, 64), F32),
            jax.ShapeDtypeStruct((2, 64, 2, 512), BF),
        ),
        in_specs=[vmem] * 4,
        out_specs=(vmem, vmem),
    )(guided, latents, conv_weight.reshape(48, 512), conv_bias.reshape(1, 512))


def solution(mesh):
    return jax.shard_map(
        shards,
        mesh=mesh,
        in_specs=(
            P("cfg", "blk", "sp", None),
            P("cfg", "blk", "sp", None),
            P("cfg", None, None, None, None),
            P("cfg"),
            P("cfg", None),
            P("cfg", None),
            P(),
            P("cfg", None, None),
            P(),
            P("blk", "sp", None),
            P(),
            P(),
        ),
        out_specs=(P("blk", "sp", None), P("blk", "sp", "cfg", None)),
        check_vma=False,
    )
```

```python
import functools
import math

import jax
import jax.numpy as jnp
from jax import lax
from jax.experimental import pallas as pl
from jax.experimental.pallas import tpu as pltpu
from jax.sharding import PartitionSpec as P

D = 3072
H = 24
HD = 128
G = 3
TXT = 256
ROWS = 128
QB = 256
MESH = pl.DeviceIdType.MESH
SCALE = math.log2(math.e) / math.sqrt(HD)
BF = jnp.bfloat16
F32 = jnp.float32

guidance_scale = 6.0
sigma_last = 0.125
vae_factor = 0.476986
norm_eps = 1e-06


def wait_bytes(ref, sem):
    pltpu.make_async_copy(ref, ref, sem).wait()


def body(
    qkv, residual, text_kv, tlen, keep, gate, w_out, fmod, w_fin, noisy,
    guided_out, latents,
    qb, kv, ob, att, po, pr, so, sr, ta, tb, mo, mb, wo, res, wf, proj, mod, pb, lat, halo, acc, m_s, l_s,
    snd, rcv_q, rcv_k, rcv_v, ysnd, yrcv, qsnd, qrcv, dsnd, drcv, psnd, prcv, osnd, orcv, lsem, tsnd, trcv, xsnd, xrcv, gsnd, grcv, hsnd, hrcv,
):
    c = lax.axis_index("cfg")
    b = lax.axis_index("blk")
    s = lax.axis_index("sp")
    xl = b // 4
    y = b % 4
    to_q = (c, xl * 4 + y + 1 - 2 * (y % 2), s)
    to_k = (c, xl * 4 + 3 - y, s)
    to_core = (1 - c, b, s)
    moved = c != xl

    def peer(d):
        return (xl, c * 4 + y, d)

    def remote(src, dst, send, recv, dev):
        return pltpu.make_async_remote_copy(src, dst, send, recv, device_id=dev, device_id_type=MESH)

    fetch_w = pltpu.make_async_copy(w_out, wo, lsem.at[0])
    fetch_r = pltpu.make_async_copy(residual.at[0], res, lsem.at[1])
    fetch_f = pltpu.make_async_copy(w_fin, wf, lsem.at[2])

    bar = pltpu.get_barrier_semaphore()

    def sig(dev):
        pl.semaphore_signal(bar, inc=1, device_id=dev, device_id_type=MESH)

    sig(to_q)
    sig(to_k)
    sig(to_core)
    for j in range(1, 8):
        sig(peer((s + j) % 8))

    @pl.when(moved)
    def _():
        sig(peer(s))

    @pl.when(b < 7)
    def _():
        sig((c, b + 1, s))

    @pl.when(b > 0)
    def _():
        sig((c, b - 1, s))

    kept = (lax.broadcasted_iota(jnp.int32, (1, TXT), 1) < tlen[0]) & (keep[...] == 1)
    mo[...] = jnp.broadcast_to(jnp.where(kept, 0.0, -1e30).astype(F32), (8, TXT))

    count = 10 + jnp.where(moved, 1, 0) + jnp.where(b < 7, 1, 0) + jnp.where(b > 0, 1, 0)
    pl.semaphore_wait(bar, count)

    rcvs = (rcv_q, rcv_k, rcv_v)

    def send_head(h):
        for kind in (1, 2, 0):
            landing = qb.at[h, 0, s] if kind == 0 else kv.at[h, 0, xl, kind - 1, s]

            def piece(d):
                return qkv.at[0, :, :, pl.ds(pl.multiple_of(kind * D + (d * G + h) * HD, HD), HD)]

            def one(j, carry):
                d = (s + j) % 8
                remote(piece(d), landing, snd.at[h, kind], rcvs[kind].at[h], peer(d)).start()
                return carry

            lax.fori_loop(1, 8, one, 0)

            @pl.when(moved)
            def _():
                remote(piece(s), landing, snd.at[h, kind], rcvs[kind].at[h], peer(s)).start()

            @pl.when(jnp.logical_not(moved))
            def _():
                pltpu.make_async_copy(piece(s), landing, rcvs[kind].at[h]).start()

    def share_half(h, half, kind):
        part = pl.ds(4 * half, 4)
        mine = kv.at[h, 0, c, kind, part]
        remote(mine, kv.at[h, 1, c, kind, part], ysnd.at[h, half, kind], yrcv.at[h, half, kind], to_k).start()

    def share_keys(h, by_half=False):
        for kind in range(2):
            mine = kv.at[h, 0, c, kind]
            wait_bytes(mine, (rcv_k, rcv_v)[kind].at[h])
            if not by_half:
                share_half(h, 0, kind)
                share_half(h, 1, kind)
            remote(mine, mine, dsnd.at[h, 0, kind], drcv.at[h, 0, kind], to_core).start()
        if by_half:
            for half in range(2):
                for kind in range(2):
                    share_half(h, half, kind)

    def share_queries(h):
        wait_bytes(qb.at[h, 0], rcv_q.at[h])
        remote(qb.at[h, 0], qb.at[h, 1], qsnd.at[h], qrcv.at[h], to_q).start()

    def pass_far(h, half):
        for kind in range(2):
            far = kv.at[h, 1, c, kind, pl.ds(4 * half, 4)]
            wait_bytes(far, yrcv.at[h, half, kind])
            remote(far, far, dsnd.at[h, 1 + half, kind], drcv.at[h, 1 + half, kind], to_core).start()

    def wait_own(h):
        for kind in range(2):
            wait_bytes(kv.at[h, 0, 1 - c, kind], drcv.at[h, 0, kind])

    def wait_far(h, half):
        for kind in range(2):
            wait_bytes(kv.at[h, 1, 1 - c, kind, pl.ds(4 * half, 4)], drcv.at[h, 1 + half, kind])

    fetch_t = pltpu.make_async_copy(text_kv.at[0], ta, lsem.at[3])
    mask_own = pltpu.make_async_copy(mo, mb.at[c], lsem.at[4])
    mask_out = remote(mo, mb.at[c], tsnd.at[1], trcv.at[1], to_core)

    def take_text(kind):
        def some(n, carry):
            tokens = pl.ds(pl.multiple_of(n * 32, 32), 32)
            found = ta[tokens, kind].astype(F32)
            head = lax.broadcasted_iota(jnp.int32, (32, H, HD), 1)
            for g in range(G):
                row = jnp.sum(jnp.where(head == s * G + g, found, 0.0), axis=1)
                tb[c, kind, g, tokens] = row.astype(BF)
            return carry

        lax.fori_loop(0, TXT // 32, some, 0)
        remote(tb.at[c, kind], tb.at[c, kind], xsnd.at[kind], xrcv.at[kind], to_core).start()

    fetch_t.start()
    send_head(0)
    mask_own.start()
    mask_out.start()
    send_head(1)
    fetch_t.wait()
    take_text(0)
    share_keys(0)
    send_head(2)
    take_text(1)
    fetch_w.start()
    fetch_r.start()
    fetch_f.start()

    blocks = 1024 // QB

    def place(u):
        return (u + s // 2) % blocks

    def rows_of(u):
        return pl.ds(pl.multiple_of(place(u) * QB, QB), QB)

    def queries(h, r, u):
        return qb[h, r, pl.ds(2 * place(u), 2)].reshape(QB, HD)

    def scores(q, keys):
        return lax.dot_general(q, keys, (((1,), (1,)), ((), ())), preferred_element_type=F32)

    def weigh(weights, values):
        padded = jnp.concatenate([values, jnp.ones_like(values)], axis=1)
        return jnp.dot(weights.astype(BF), padded, preferred_element_type=F32)

    def softmax_blocks(h, far, rowsets, done=None, half=None):
        part = slice(0, 8) if half is None else slice(4 * half, 4 * half + 4)
        keys = kv[h, far, :, 0, part].reshape(-1, HD)
        values = kv[h, far, :, 1, part].reshape(-1, HD)
        with_text = far == 0 and rowsets == (0,)
        if with_text:
            text_keys = tb[xl, 0, h]
            text_values = tb[xl, 1, h]
            added = mb[xl]
        par = h % 2
        order = [(r, u) for r in rowsets for u in range(blocks)]

        def all_scores(r, u):
            q = queries(h, r, u)
            if not with_text:
                return scores(q, keys), None
            return scores(q, keys), scores(q, text_keys) + added[0:1]

        ahead = all_scores(*order[0])
        for i, (r, u) in enumerate(order):
            now, now_text = ahead
            if i + 1 < len(order):
                ahead = all_scores(*order[i + 1])
            rows = rows_of(u)
            top = jnp.max(now, axis=1, keepdims=True)
            if far == 0:
                if with_text:
                    top = jnp.maximum(top, jnp.max(now_text, axis=1, keepdims=True))
                new = jnp.broadcast_to(top, (QB, HD))
                out = weigh(jnp.exp2((now - top) * SCALE), values)
                if with_text:
                    out = out + weigh(jnp.exp2((now_text - top) * SCALE), text_values)
                total, weight = out[:, :HD], out[:, HD:]
            else:
                old = m_s[par, r, rows]
                new = jnp.maximum(old, top)
                factor = jnp.exp2((old - new) * SCALE)
                out = weigh(jnp.exp2((now - new[:, :1]) * SCALE), values)
                total = acc[par, r, rows] * factor + out[:, :HD]
                weight = l_s[par, r, rows] * factor + out[:, HD:]
            if r == 1 and far == 1 and done is not None:
                done(u, new, total, weight)
            else:
                m_s[par, r, rows] = new
                acc[par, r, rows] = total
                l_s[par, r, rows] = weight

    def send_partial(h):
        def done(i, top, total, weight):
            u = place(i)
            cols = rows_of(i)
            po[h, pl.ds(2 * u, 2)] = (total / weight).astype(BF).reshape(2, 2, 64, HD)
            lane = lax.broadcasted_iota(jnp.int32, (QB, HD), 1)
            so[h, u] = jnp.where(lane == 0, top, weight).T[0:8]
            part = po.at[h, pl.ds(2 * u, 2)]
            remote(part, pr.at[h, pl.ds(2 * u, 2)], psnd.at[h, 0, u], prcv.at[h, 0, u], to_q).start()
            remote(so.at[h, u], sr.at[h, u], psnd.at[h, 1, u], prcv.at[h, 1, u], to_q).start()

        return done

    def join(h):
        par = h % 2

        def block(j, carry):
            u = place(j)
            rows = rows_of(j)
            wait_bytes(pr.at[h, pl.ds(2 * u, 2)], prcv.at[h, 0, u])
            wait_bytes(sr.at[h, u], prcv.at[h, 1, u])
            stats = sr[h, u].T
            top_p = stats[:, 0:1]
            sum_p = stats[:, 1:2]
            top_a = m_s[par, 0, rows]
            new = jnp.maximum(top_a, top_p)
            f_a = jnp.exp2((top_a - new) * SCALE)
            f_p = jnp.exp2((top_p - new) * SCALE) * sum_p
            partial = pr[h, pl.ds(2 * u, 2)].reshape(QB, HD).astype(F32)
            out = (acc[par, 0, rows] * f_a + partial * f_p) / (l_s[par, 0, rows] * f_a + f_p)
            ob[h, pl.ds(2 * u, 2)] = out.astype(BF).reshape(2, 2, 64, HD)
            for k in range(2):
                d = 2 * u + k

                @pl.when(jnp.logical_or(moved, d != s))
                def _():
                    remote(ob.at[h, d], att.at[s, h], osnd.at[h], orcv.at[h], peer(d)).start()

                @pl.when(jnp.logical_not(jnp.logical_or(moved, d != s)))
                def _():
                    pltpu.make_async_copy(ob.at[h, d], att.at[s, h], orcv.at[h]).start()

            return carry

        lax.fori_loop(0, blocks, block, 0)

    def project(h):
        wait_bytes(att.at[:, h], orcv.at[h])
        rows = jnp.concatenate([att[d, h].reshape(ROWS, HD) for d in range(8)], axis=1)

        def columns(n, carry):
            cols = pl.ds(pl.multiple_of(n * 512, 512), 512)
            weight = jnp.concatenate(
                [wo[pl.ds(pl.multiple_of((d * G + h) * HD, HD), HD), cols] for d in range(8)], axis=0
            )
            proj[:, cols] += jnp.dot(rows, weight, preferred_element_type=F32)
            return carry

        lax.fori_loop(0, D // 512, columns, 0)

    def own_step(h):
        wait_own(h)
        softmax_blocks(h, 0, (0,))

    def shared_step(h):
        wait_bytes(qb.at[h, 1], qrcv.at[h])
        softmax_blocks(h, 0, (1,))

    proj[...] = jnp.zeros_like(proj)
    mask_own.wait()
    share_queries(0)
    for kind in range(2):
        wait_bytes(tb.at[1 - c, kind], xrcv.at[kind])
    wait_bytes(mb.at[1 - c], trcv.at[1])
    own_step(0)
    share_keys(1)
    pass_far(0, 0)
    pass_far(0, 1)
    shared_step(0)

    def step(h, carry):
        share_queries(h + 1)
        own_step(h + 1)
        wait_far(h, 0)
        wait_far(h, 1)
        softmax_blocks(h, 1, (1, 0), send_partial(h))

        @pl.when(h == 0)
        def _():
            share_keys(2, True)
            pass_far(1, 0)
            pass_far(1, 1)

        @pl.when(h == 1)
        def _():
            pass_far(2, 0)

        shared_step(h + 1)
        join(h)
        return carry

    lax.fori_loop(0, 2, step, 0)
    pass_far(2, 1)
    fetch_w.wait()
    project(0)
    wait_far(2, 0)
    softmax_blocks(2, 1, (1,), None, 0)
    wait_far(2, 1)
    softmax_blocks(2, 1, (1,), send_partial(2), 1)
    softmax_blocks(2, 1, (0,))
    project(1)
    join(2)

    def wait_out(h):
        wait_bytes(ob.at[h, pl.ds(0, 7)], osnd.at[h])

        @pl.when(moved)
        def _():
            wait_bytes(ob.at[h, 0], osnd.at[h])

    for h in range(G):
        for kind in range(3):
            wait_bytes(qb.at[h, 0, pl.ds(0, 7)], snd.at[h, kind])

            @pl.when(moved)
            def _():
                wait_bytes(qb.at[h, 0, 0], snd.at[h, kind])

        wait_bytes(qb.at[h, 0], qsnd.at[h])
        for kind in range(2):
            wait_bytes(kv.at[h, 0, c, 0], dsnd.at[h, 0, kind])
            for half in range(2):
                wait_bytes(kv.at[h, 0, c, 0, pl.ds(0, 4)], ysnd.at[h, half, kind])
                wait_bytes(kv.at[h, 0, c, 0, pl.ds(0, 4)], dsnd.at[h, 1 + half, kind])
        for u in range(blocks):
            wait_bytes(po.at[h, pl.ds(0, 2)], psnd.at[h, 0, u])
            wait_bytes(so.at[h, 0], psnd.at[h, 1, u])
    for kind in range(2):
        wait_bytes(tb.at[c, kind], xsnd.at[kind])
    wait_bytes(mb.at[c], tsnd.at[1])
    wait_out(0)
    wait_out(1)
    project(G - 1)

    fetch_r.wait()
    fetch_f.wait()

    def norm(n, carry):
        rows = pl.ds(pl.multiple_of(n * 32, 32), 32)
        shown = res[n // 2, pl.ds(pl.multiple_of((n % 2) * 32, 32), 32)].astype(F32)
        hidden = shown + gate[...] * proj[rows]
        centered = hidden - jnp.mean(hidden, axis=1, keepdims=True)
        normed = centered * lax.rsqrt(jnp.mean(centered * centered, axis=1, keepdims=True) + norm_eps)
        mod[rows] = (normed * (1.0 + fmod[0, 1:2]) + fmod[0, 0:1]).astype(BF)
        return carry

    lax.fori_loop(0, 4, norm, 0)
    pb[c] = lax.dot_general(mod[...], wf[...], (((1,), (1,)), ((), ())), preferred_element_type=F32)
    remote(pb.at[c], pb.at[c], gsnd, grcv, to_core).start()
    wait_bytes(pb.at[1 - c], grcv)
    uncond = pb[1]
    guided = uncond + guidance_scale * (pb[0] - uncond)
    guided_out[...] = guided
    lat[...] = ((noisy[...] - sigma_last * guided) / vae_factor).astype(BF)

    @pl.when(b < 7)
    def _():
        remote(lat, halo, hsnd, hrcv, (c, b + 1, s)).start()

    latents[1] = lat[...]

    @pl.when(b == 0)
    def _():
        latents[0] = jnp.zeros_like(halo)

    @pl.when(b > 0)
    def _():
        wait_bytes(halo, hrcv)
        latents[0] = halo[...]

    wait_out(2)
    wait_bytes(pb.at[c], gsnd)

    @pl.when(b < 7)
    def _():
        wait_bytes(lat, hsnd)


def conv_body(guided, latents, conv_w, conv_b, velocity, decoded):
    c = lax.axis_index("cfg")
    velocity[...] = guided[...].reshape(2, 64, 64)
    before = latents[0]
    here = latents[1]
    across = jnp.concatenate([before[64:], here[:64]], axis=0)
    entry = lax.broadcasted_iota(jnp.int32, (64, 48), 0)
    place = lax.broadcasted_iota(jnp.int32, (64, 48), 1)
    outs = []
    for i in range(2):
        taps = jnp.zeros((ROWS, 48), F32)
        for t, frames in enumerate((before, across, here)):
            chosen = (entry == 4 * (place - 16 * t) + 2 * c + i) & (place >= 16 * t) & (place < 16 * t + 16)
            taps = taps + jnp.dot(frames, jnp.where(chosen, 1.0, 0.0).astype(BF), preferred_element_type=F32)
        out = jnp.dot(taps.astype(BF), conv_w[...], preferred_element_type=F32) + conv_b[...]
        outs.append(out.reshape(2, 64, 512))
    decoded[...] = jnp.stack(outs, axis=2).astype(BF)


def shards(qkv, residual, text_kv, text_len, text_keep, attn_gate, w_out, final_mod, w_final, noisy, conv_weight, conv_bias):
    hbm = pl.BlockSpec(memory_space=pl.ANY)
    vmem = pl.BlockSpec(memory_space=pltpu.VMEM)
    smem = pl.BlockSpec(memory_space=pltpu.SMEM)
    dma = pltpu.SemaphoreType.DMA
    guided, latents = pl.pallas_call(
        body,
        out_shape=(
            jax.ShapeDtypeStruct((ROWS, 64), F32),
            jax.ShapeDtypeStruct((2, ROWS, 64), BF),
        ),
        in_specs=[hbm, hbm, hbm, smem, vmem, vmem, hbm, vmem, hbm, vmem],
        out_specs=(vmem, vmem),
        scratch_shapes=[
            pltpu.VMEM((G, 2, 8, 2, 64, HD), BF),
            pltpu.VMEM((G, 2, 2, 2, 8, 2, 64, HD), BF),
            pltpu.VMEM((G, 8, 2, 64, HD), BF),
            pltpu.VMEM((8, G, 2, 64, HD), BF),
            pltpu.VMEM((G, 8, 2, 64, HD), BF),
            pltpu.VMEM((G, 8, 2, 64, HD), BF),
            pltpu.VMEM((G, 4, 8, QB), F32),
            pltpu.VMEM((G, 4, 8, QB), F32),
            pltpu.VMEM((TXT, 2, H, HD), BF),
            pltpu.VMEM((2, 2, G, TXT, HD), BF),
            pltpu.VMEM((8, TXT), F32),
            pltpu.VMEM((2, 8, TXT), F32),
            pltpu.VMEM((D, D), BF),
            pltpu.VMEM((2, 64, D), BF),
            pltpu.VMEM((64, D), BF),
            pltpu.VMEM((ROWS, D), F32),
            pltpu.VMEM((ROWS, D), BF),
            pltpu.VMEM((2, ROWS, 64), F32),
            pltpu.VMEM((ROWS, 64), BF),
            pltpu.VMEM((ROWS, 64), BF),
            pltpu.VMEM((2, 2, 1024, HD), F32),
            pltpu.VMEM((2, 2, 1024, HD), F32),
            pltpu.VMEM((2, 2, 1024, HD), F32),
            dma((G, 3)),
            dma((G,)),
            dma((G,)),
            dma((G,)),
            dma((G, 2, 2)),
            dma((G, 2, 2)),
            dma((G,)),
            dma((G,)),
            dma((G, 3, 2)),
            dma((G, 3, 2)),
            dma((G, 2, 4)),
            dma((G, 2, 4)),
            dma((G,)),
            dma((G,)),
            dma((5,)),
            dma((2,)),
            dma((2,)),
            dma((2,)),
            dma((2,)),
            dma,
            dma,
            dma,
            dma,
        ],
        compiler_params=pltpu.CompilerParams(
            collective_id=0, has_side_effects=True, vmem_limit_bytes=60 * 2**20
        ),
    )(
        qkv,
        residual,
        text_kv,
        text_len,
        text_keep,
        attn_gate,
        w_out,
        final_mod,
        w_final.T,
        noisy.reshape(ROWS, 64),
    )
    return pl.pallas_call(
        conv_body,
        out_shape=(
            jax.ShapeDtypeStruct((2, 64, 64), F32),
            jax.ShapeDtypeStruct((2, 64, 2, 512), BF),
        ),
        in_specs=[vmem] * 4,
        out_specs=(vmem, vmem),
    )(guided, latents, conv_weight.reshape(48, 512), conv_bias.reshape(1, 512))


def solution(mesh):
    return jax.shard_map(
        shards,
        mesh=mesh,
        in_specs=(
            P("cfg", "blk", "sp", None),
            P("cfg", "blk", "sp", None),
            P("cfg", None, None, None, None),
            P("cfg"),
            P("cfg", None),
            P("cfg", None),
            P(),
            P("cfg", None, None),
            P(),
            P("blk", "sp", None),
            P(),
            P(),
        ),
        out_specs=(P("blk", "sp", None), P("blk", "sp", "cfg", None)),
        check_vma=False,
    )
```

```python
import functools
import math

import jax
import jax.numpy as jnp
from jax import lax
from jax.experimental import pallas as pl
from jax.experimental.pallas import tpu as pltpu
from jax.sharding import PartitionSpec as P

D = 3072
H = 24
HD = 128
G = 3
TXT = 256
ROWS = 128
QB = 256
MESH = pl.DeviceIdType.MESH
SCALE = math.log2(math.e) / math.sqrt(HD)
BF = jnp.bfloat16
F32 = jnp.float32

guidance_scale = 6.0
sigma_last = 0.125
vae_factor = 0.476986
norm_eps = 1e-06


def wait_bytes(ref, sem):
    pltpu.make_async_copy(ref, ref, sem).wait()


def body(
    qkv, residual, text_kv, tlen, keep, gate, w_out, fmod, w_fin, noisy,
    guided_out, latents,
    qb, kv, ob, att, ta, tb, mo, mb, wo, res, wf, proj, mod, pb, lat, halo, acc, m_s, l_s,
    snd, rcv_q, rcv_k, rcv_v, ysnd, yrcv, qsnd, qrcv, dsnd, drcv, osnd, orcv, lsem, tsnd, trcv, xsnd, xrcv, gsnd, grcv, hsnd, hrcv,
):
    c = lax.axis_index("cfg")
    b = lax.axis_index("blk")
    s = lax.axis_index("sp")
    xl = b // 4
    y = b % 4
    yq = y + 1 - 2 * (y % 2)
    to_q = (c, xl * 4 + yq, s)
    to_k = (c, xl * 4 + 3 - y, s)
    to_core = (1 - c, b, s)
    moved = c != xl

    def peer(d):
        return (xl, c * 4 + y, d)

    def owner(r, d):
        return (xl, c * 4 + (yq if r else y), d)

    def remote(src, dst, send, recv, dev):
        return pltpu.make_async_remote_copy(src, dst, send, recv, device_id=dev, device_id_type=MESH)

    fetch_w = pltpu.make_async_copy(w_out, wo, lsem.at[0])
    fetch_r = pltpu.make_async_copy(residual.at[0], res, lsem.at[1])
    fetch_f = pltpu.make_async_copy(w_fin, wf, lsem.at[2])

    bar = pltpu.get_barrier_semaphore()

    def sig(dev):
        pl.semaphore_signal(bar, inc=1, device_id=dev, device_id_type=MESH)

    sig(to_q)
    sig(to_k)
    sig(to_core)
    for j in range(1, 8):
        sig(peer((s + j) % 8))
    for j in range(8):
        sig(owner(1, (s + j) % 8))

    @pl.when(moved)
    def _():
        sig(peer(s))

    @pl.when(b < 7)
    def _():
        sig((c, b + 1, s))

    @pl.when(b > 0)
    def _():
        sig((c, b - 1, s))

    kept = (lax.broadcasted_iota(jnp.int32, (1, TXT), 1) < tlen[...]) & (keep[...] == 1)
    mo[...] = jnp.broadcast_to(jnp.where(kept, 0.0, -1e30).astype(F32), (8, TXT))

    count = 18 + jnp.where(moved, 1, 0) + jnp.where(b < 7, 1, 0) + jnp.where(b > 0, 1, 0)
    pl.semaphore_wait(bar, count)

    rcvs = (rcv_q, rcv_k, rcv_v)

    def send_head(h):
        for kind in (1, 2, 0):
            landing = qb.at[h, 0, s] if kind == 0 else kv.at[h, 0, xl, kind - 1, s]

            def piece(d):
                return qkv.at[0, :, :, pl.ds(pl.multiple_of(kind * D + (d * G + h) * HD, HD), HD)]

            def one(j, carry):
                d = (s + j) % 8
                remote(piece(d), landing, snd.at[h, kind], rcvs[kind].at[h], peer(d)).start()
                return carry

            lax.fori_loop(1, 8, one, 0)

            @pl.when(moved)
            def _():
                remote(piece(s), landing, snd.at[h, kind], rcvs[kind].at[h], peer(s)).start()

            @pl.when(jnp.logical_not(moved))
            def _():
                pltpu.make_async_copy(piece(s), landing, rcvs[kind].at[h]).start()

    def share_half(h, half, kind):
        part = pl.ds(4 * half, 4)
        mine = kv.at[h, 0, c, kind, part]
        remote(mine, kv.at[h, 1, c, kind, part], ysnd.at[h, half, kind], yrcv.at[h, half, kind], to_k).start()

    def share_keys(h, by_half=False):
        for kind in range(2):
            mine = kv.at[h, 0, c, kind]
            wait_bytes(mine, (rcv_k, rcv_v)[kind].at[h])
            if not by_half:
                share_half(h, 0, kind)
                share_half(h, 1, kind)
            remote(mine, mine, dsnd.at[h, 0, kind], drcv.at[h, 0, kind], to_core).start()
        if by_half:
            for half in range(2):
                for kind in range(2):
                    share_half(h, half, kind)

    def share_queries(h):
        wait_bytes(qb.at[h, 0], rcv_q.at[h])
        remote(qb.at[h, 0], qb.at[h, 1], qsnd.at[h], qrcv.at[h], to_q).start()

    def pass_far(h, half):
        for kind in range(2):
            far = kv.at[h, 1, c, kind, pl.ds(4 * half, 4)]
            wait_bytes(far, yrcv.at[h, half, kind])
            remote(far, far, dsnd.at[h, 1 + half, kind], drcv.at[h, 1 + half, kind], to_core).start()

    def wait_own(h):
        for kind in range(2):
            wait_bytes(kv.at[h, 0, 1 - c, kind], drcv.at[h, 0, kind])

    def wait_far(h, half):
        for kind in range(2):
            wait_bytes(kv.at[h, 1, 1 - c, kind, pl.ds(4 * half, 4)], drcv.at[h, 1 + half, kind])

    fetch_t = pltpu.make_async_copy(text_kv.at[0], ta, lsem.at[3])
    mask_own = pltpu.make_async_copy(mo, mb.at[c], lsem.at[4])
    mask_out = remote(mo, mb.at[c], tsnd.at[1], trcv.at[1], to_core)

    def take_text(kind):
        def some(n, carry):
            tokens = pl.ds(pl.multiple_of(n * 32, 32), 32)
            found = ta[tokens, kind].astype(F32)
            head = lax.broadcasted_iota(jnp.int32, (32, H, HD), 1)
            for g in range(G):
                row = jnp.sum(jnp.where(head == s * G + g, found, 0.0), axis=1)
                tb[c, kind, g, tokens] = row.astype(BF)
            return carry

        lax.fori_loop(0, TXT // 32, some, 0)
        remote(tb.at[c, kind], tb.at[c, kind], xsnd.at[kind], xrcv.at[kind], to_core).start()

    fetch_t.start()
    send_head(0)
    mask_own.start()
    mask_out.start()
    send_head(1)
    fetch_t.wait()
    take_text(0)
    share_keys(0)
    send_head(2)
    take_text(1)
    fetch_w.start()
    fetch_r.start()
    fetch_f.start()

    blocks = 1024 // QB

    def place(u):
        return (u + s // 2) % blocks

    def rows_of(u):
        return pl.ds(pl.multiple_of(place(u) * QB, QB), QB)

    def queries(h, r, u):
        return qb[h, r, pl.ds(2 * place(u), 2)].reshape(QB, HD)

    def scores(q, keys):
        return lax.dot_general(q, keys, (((1,), (1,)), ((), ())), preferred_element_type=F32)

    def weigh(weights, values):
        padded = jnp.concatenate([values, jnp.ones_like(values)], axis=1)
        return jnp.dot(weights.astype(BF), padded, preferred_element_type=F32)

    def softmax_blocks(h, far, rowsets, done=None, half=None):
        part = slice(0, 8) if half is None else slice(4 * half, 4 * half + 4)
        keys = kv[h, far, :, 0, part].reshape(-1, HD)
        values = kv[h, far, :, 1, part].reshape(-1, HD)
        with_text = far == 0 and rowsets == (0,)
        if with_text:
            text_keys = tb[xl, 0, h]
            text_values = tb[xl, 1, h]
            added = mb[xl]
        par = h % 2
        order = [(r, u) for r in rowsets for u in range(blocks)]

        def all_scores(r, u):
            q = queries(h, r, u)
            if not with_text:
                return scores(q, keys), None
            return scores(q, keys), scores(q, text_keys) + added[0:1]

        ahead = all_scores(*order[0])
        for i, (r, u) in enumerate(order):
            now, now_text = ahead
            if i + 1 < len(order):
                ahead = all_scores(*order[i + 1])
            rows = rows_of(u)
            top = jnp.max(now, axis=1, keepdims=True)
            if far == 0:
                if with_text:
                    top = jnp.maximum(top, jnp.max(now_text, axis=1, keepdims=True))
                new = jnp.broadcast_to(top, (QB, HD))
                out = weigh(jnp.exp2((now - top) * SCALE), values)
                if with_text:
                    out = out + weigh(jnp.exp2((now_text - top) * SCALE), text_values)
                total, weight = out[:, :HD], out[:, HD:]
            else:
                old = m_s[par, r, rows]
                new = jnp.maximum(old, top)
                factor = jnp.exp2((old - new) * SCALE)
                out = weigh(jnp.exp2((now - new[:, :1]) * SCALE), values)
                total = acc[par, r, rows] * factor + out[:, :HD]
                weight = l_s[par, r, rows] * factor + out[:, HD:]
            if done is not None:
                done(r, u, new, total, weight)
            else:
                m_s[par, r, rows] = new
                acc[par, r, rows] = total
                l_s[par, r, rows] = weight

    def finish(h):
        def done(r, i, top, total, weight):
            out = (total / weight).astype(BF)
            lane = lax.broadcasted_iota(jnp.int32, (QB, HD), 1)
            stats = jnp.zeros((QB, HD), F32)
            for at, value, pieces in ((0, top, 3), (3, weight, 2)):
                for k in range(pieces):
                    piece = value.astype(BF).astype(F32)
                    stats = jnp.where(lane == at + k, piece, stats)
                    value = value - piece
            below = stats.T[0:16].astype(BF)
            for k in range(2):
                d = 2 * place(i) + k
                ob[r, h, d, 0:ROWS] = out[k * ROWS : (k + 1) * ROWS]
                ob[r, h, d, ROWS : ROWS + 16] = below[:, k * ROWS : (k + 1) * ROWS]

        return done

    def send_out(h, r):
        def one(j, carry):
            d = (2 * (s // 2) + j) % 8
            slab = ob.at[r, h, d]
            landing = att.at[r, s, h]
            if r:
                remote(slab, landing, osnd.at[h, 1], orcv.at[h, 1], owner(1, d)).start()
                return carry

            @pl.when(jnp.logical_or(moved, d != s))
            def _():
                remote(slab, landing, osnd.at[h, 0], orcv.at[h, 0], owner(0, d)).start()

            @pl.when(jnp.logical_not(jnp.logical_or(moved, d != s)))
            def _():
                pltpu.make_async_copy(slab, landing, orcv.at[h, 0]).start()

            return carry

        lax.fori_loop(0, 8, one, 0)

    def project(h):
        tops, sums = [], []
        for r in range(2):
            wait_bytes(att.at[r, :, h], orcv.at[h, r])
            stats = att[r, :, h, ROWS : ROWS + 16].astype(F32)
            tops.append(stats[:, 0] + stats[:, 1] + stats[:, 2])
            sums.append(stats[:, 3] + stats[:, 4])
        top = jnp.maximum(tops[0], tops[1])
        parts = [jnp.exp2((tops[r] - top) * SCALE) * sums[r] for r in range(2)]
        whole = parts[0] + parts[1]
        shares = [(part / whole).T for part in parts]
        rows = jnp.concatenate(
            [
                sum(att[r, d, h, 0:ROWS].astype(F32) * shares[r][:, d : d + 1] for r in range(2)).astype(BF)
                for d in range(8)
            ],
            axis=1,
        )

        def columns(n, carry):
            cols = pl.ds(pl.multiple_of(n * 512, 512), 512)
            weight = jnp.concatenate(
                [wo[pl.ds(pl.multiple_of((d * G + h) * HD, HD), HD), cols] for d in range(8)], axis=0
            )
            proj[:, cols] += jnp.dot(rows, weight, preferred_element_type=F32)
            return carry

        lax.fori_loop(0, D // 512, columns, 0)

    def own_step(h):
        wait_own(h)
        softmax_blocks(h, 0, (0,))

    def shared_step(h):
        wait_bytes(qb.at[h, 1], qrcv.at[h])
        softmax_blocks(h, 0, (1,))

    proj[...] = jnp.zeros_like(proj)
    mask_own.wait()
    share_queries(0)
    for kind in range(2):
        wait_bytes(tb.at[1 - c, kind], xrcv.at[kind])
    wait_bytes(mb.at[1 - c], trcv.at[1])
    own_step(0)
    share_keys(1)
    pass_far(0, 0)
    pass_far(0, 1)
    shared_step(0)

    def step(h, carry):
        share_queries(h + 1)
        own_step(h + 1)
        wait_far(h, 0)
        wait_far(h, 1)
        softmax_blocks(h, 1, (1, 0), finish(h))
        send_out(h, 1)
        send_out(h, 0)

        @pl.when(h == 0)
        def _():
            share_keys(2, True)
            pass_far(1, 0)
            pass_far(1, 1)

        @pl.when(h == 1)
        def _():
            pass_far(2, 0)

        shared_step(h + 1)
        return carry

    lax.fori_loop(0, 2, step, 0)
    pass_far(2, 1)
    fetch_w.wait()
    project(0)
    wait_far(2, 0)
    softmax_blocks(2, 1, (1, 0), None, 0)
    wait_far(2, 1)
    softmax_blocks(2, 1, (1,), finish(2), 1)
    send_out(2, 1)
    softmax_blocks(2, 1, (0,), finish(2), 1)
    send_out(2, 0)
    project(1)

    def wait_out(h):
        wait_bytes(ob.at[1, h], osnd.at[h, 1])
        wait_bytes(ob.at[0, h, pl.ds(0, 7)], osnd.at[h, 0])

        @pl.when(moved)
        def _():
            wait_bytes(ob.at[0, h, 0], osnd.at[h, 0])

    for h in range(G):
        for kind in range(3):
            wait_bytes(qb.at[h, 0, pl.ds(0, 7)], snd.at[h, kind])

            @pl.when(moved)
            def _():
                wait_bytes(qb.at[h, 0, 0], snd.at[h, kind])

        wait_bytes(qb.at[h, 0], qsnd.at[h])
        for kind in range(2):
            wait_bytes(kv.at[h, 0, c, 0], dsnd.at[h, 0, kind])
            for half in range(2):
                wait_bytes(kv.at[h, 0, c, 0, pl.ds(0, 4)], ysnd.at[h, half, kind])
                wait_bytes(kv.at[h, 0, c, 0, pl.ds(0, 4)], dsnd.at[h, 1 + half, kind])
    for kind in range(2):
        wait_bytes(tb.at[c, kind], xsnd.at[kind])
    wait_bytes(mb.at[c], tsnd.at[1])
    wait_out(0)
    wait_out(1)
    project(G - 1)

    fetch_r.wait()
    fetch_f.wait()

    def norm(n, carry):
        rows = pl.ds(pl.multiple_of(n * 32, 32), 32)
        shown = res[n // 2, pl.ds(pl.multiple_of((n % 2) * 32, 32), 32)].astype(F32)
        hidden = shown + gate[...] * proj[rows]
        centered = hidden - jnp.mean(hidden, axis=1, keepdims=True)
        normed = centered * lax.rsqrt(jnp.mean(centered * centered, axis=1, keepdims=True) + norm_eps)
        mod[rows] = (normed * (1.0 + fmod[0, 1:2]) + fmod[0, 0:1]).astype(BF)
        return carry

    lax.fori_loop(0, 4, norm, 0)
    pb[c] = lax.dot_general(mod[...], wf[...], (((1,), (1,)), ((), ())), preferred_element_type=F32)
    remote(pb.at[c], pb.at[c], gsnd, grcv, to_core).start()
    wait_bytes(pb.at[1 - c], grcv)
    uncond = pb[1]
    guided = uncond + guidance_scale * (pb[0] - uncond)
    guided_out[...] = guided
    lat[...] = ((noisy[...] - sigma_last * guided) / vae_factor).astype(BF)

    @pl.when(b < 7)
    def _():
        remote(lat, halo, hsnd, hrcv, (c, b + 1, s)).start()

    latents[1] = lat[...]

    @pl.when(b == 0)
    def _():
        latents[0] = jnp.zeros_like(halo)

    @pl.when(b > 0)
    def _():
        wait_bytes(halo, hrcv)
        latents[0] = halo[...]

    wait_out(2)
    wait_bytes(pb.at[c], gsnd)

    @pl.when(b < 7)
    def _():
        wait_bytes(lat, hsnd)


def conv_body(guided, latents, conv_w, conv_b, velocity, decoded):
    c = lax.axis_index("cfg")
    velocity[...] = guided[...].reshape(2, 64, 64)
    before = latents[0]
    here = latents[1]
    across = jnp.concatenate([before[64:], here[:64]], axis=0)
    entry = lax.broadcasted_iota(jnp.int32, (64, 48), 0)
    place = lax.broadcasted_iota(jnp.int32, (64, 48), 1)
    outs = []
    for i in range(2):
        taps = jnp.zeros((ROWS, 48), F32)
        for t, frames in enumerate((before, across, here)):
            chosen = (entry == 4 * (place - 16 * t) + 2 * c + i) & (place >= 16 * t) & (place < 16 * t + 16)
            taps = taps + jnp.dot(frames, jnp.where(chosen, 1.0, 0.0).astype(BF), preferred_element_type=F32)
        out = jnp.dot(taps.astype(BF), conv_w[...], preferred_element_type=F32) + conv_b[...]
        outs.append(out.reshape(2, 64, 512))
    decoded[...] = jnp.stack(outs, axis=2).astype(BF)


def shards(qkv, residual, text_kv, text_len, text_keep, attn_gate, w_out, final_mod, w_final, noisy, conv_weight, conv_bias):
    hbm = pl.BlockSpec(memory_space=pl.ANY)
    vmem = pl.BlockSpec(memory_space=pltpu.VMEM)
    dma = pltpu.SemaphoreType.DMA
    guided, latents = pl.pallas_call(
        body,
        out_shape=(
            jax.ShapeDtypeStruct((ROWS, 64), F32),
            jax.ShapeDtypeStruct((2, ROWS, 64), BF),
        ),
        in_specs=[hbm, hbm, hbm, vmem, vmem, vmem, hbm, vmem, hbm, vmem],
        out_specs=(vmem, vmem),
        scratch_shapes=[
            pltpu.VMEM((G, 2, 8, 2, 64, HD), BF),
            pltpu.VMEM((G, 2, 2, 2, 8, 2, 64, HD), BF),
            pltpu.VMEM((2, G, 8, ROWS + 16, HD), BF),
            pltpu.VMEM((2, 8, G, ROWS + 16, HD), BF),
            pltpu.VMEM((TXT, 2, H, HD), BF),
            pltpu.VMEM((2, 2, G, TXT, HD), BF),
            pltpu.VMEM((8, TXT), F32),
            pltpu.VMEM((2, 8, TXT), F32),
            pltpu.VMEM((D, D), BF),
            pltpu.VMEM((2, 64, D), BF),
            pltpu.VMEM((64, D), BF),
            pltpu.VMEM((ROWS, D), F32),
            pltpu.VMEM((ROWS, D), BF),
            pltpu.VMEM((2, ROWS, 64), F32),
            pltpu.VMEM((ROWS, 64), BF),
            pltpu.VMEM((ROWS, 64), BF),
            pltpu.VMEM((2, 2, 1024, HD), F32),
            pltpu.VMEM((2, 2, 1024, HD), F32),
            pltpu.VMEM((2, 2, 1024, HD), F32),
            dma((G, 3)),
            dma((G,)),
            dma((G,)),
            dma((G,)),
            dma((G, 2, 2)),
            dma((G, 2, 2)),
            dma((G,)),
            dma((G,)),
            dma((G, 3, 2)),
            dma((G, 3, 2)),
            dma((G, 2)),
            dma((G, 2)),
            dma((5,)),
            dma((2,)),
            dma((2,)),
            dma((2,)),
            dma((2,)),
            dma,
            dma,
            dma,
            dma,
        ],
        compiler_params=pltpu.CompilerParams(
            collective_id=0, has_side_effects=True, vmem_limit_bytes=60 * 2**20
        ),
    )(
        qkv,
        residual,
        text_kv,
        text_len.reshape(1, 1),
        text_keep,
        attn_gate,
        w_out,
        final_mod,
        w_final.T,
        noisy.reshape(ROWS, 64),
    )
    return pl.pallas_call(
        conv_body,
        out_shape=(
            jax.ShapeDtypeStruct((2, 64, 64), F32),
            jax.ShapeDtypeStruct((2, 64, 2, 512), BF),
        ),
        in_specs=[vmem] * 4,
        out_specs=(vmem, vmem),
    )(guided, latents, conv_weight.reshape(48, 512), conv_bias.reshape(1, 512))


def solution(mesh):
    return jax.shard_map(
        shards,
        mesh=mesh,
        in_specs=(
            P("cfg", "blk", "sp", None),
            P("cfg", "blk", "sp", None),
            P("cfg", None, None, None, None),
            P("cfg"),
            P("cfg", None),
            P("cfg", None),
            P(),
            P("cfg", None, None),
            P(),
            P("blk", "sp", None),
            P(),
            P(),
        ),
        out_specs=(P("blk", "sp", None), P("blk", "sp", "cfg", None)),
        check_vma=False,
    )
```

```python
import functools
import math

import jax
import jax.numpy as jnp
from jax import lax
from jax.experimental import pallas as pl
from jax.experimental.pallas import tpu as pltpu
from jax.sharding import PartitionSpec as P

D = 3072
H = 24
HD = 128
G = 3
TXT = 256
ROWS = 128
QB = 256
MESH = pl.DeviceIdType.MESH
SCALE = math.log2(math.e) / math.sqrt(HD)
BF = jnp.bfloat16
F32 = jnp.float32

guidance_scale = 6.0
sigma_last = 0.125
vae_factor = 0.476986
norm_eps = 1e-06


def wait_bytes(ref, sem):
    pltpu.make_async_copy(ref, ref, sem).wait()


def body(
    qkv, residual, text_kv, tlen, keep, gate, w_out, fmod, w_fin, noisy,
    guided_out, latents,
    qb, kv, ob, att, ta, tb, mo, mb, wo, res, wf, proj, mod, pb, lat, halo, acc, m_s, l_s,
    snd, rcv_q, rcv_k, rcv_v, ysnd, yrcv, qsnd, qrcv, dsnd, drcv, osnd, orcv, lsem, tsnd, trcv, xsnd, xrcv, gsnd, grcv, hsnd, hrcv,
):
    c = lax.axis_index("cfg")
    b = lax.axis_index("blk")
    s = lax.axis_index("sp")
    xl = b // 4
    y = b % 4
    yq = y + 1 - 2 * (y % 2)
    to_q = (c, xl * 4 + yq, s)
    to_k = (c, xl * 4 + 3 - y, s)
    to_core = (1 - c, b, s)
    moved = c != xl

    def peer(d):
        return (xl, c * 4 + y, d)

    def owner(r, d):
        return (xl, c * 4 + (yq if r else y), d)

    def remote(src, dst, send, recv, dev):
        return pltpu.make_async_remote_copy(src, dst, send, recv, device_id=dev, device_id_type=MESH)

    fetch_w = pltpu.make_async_copy(w_out, wo, lsem.at[0])
    fetch_r = pltpu.make_async_copy(residual.at[0], res, lsem.at[1])
    fetch_f = pltpu.make_async_copy(w_fin, wf, lsem.at[2])

    bar = pltpu.get_barrier_semaphore()

    def sig(dev):
        pl.semaphore_signal(bar, inc=1, device_id=dev, device_id_type=MESH)

    sig(to_q)
    sig(to_k)
    sig(to_core)
    for j in range(1, 8):
        sig(peer((s + j) % 8))
    for j in range(8):
        sig(owner(1, (s + j) % 8))

    @pl.when(moved)
    def _():
        sig(peer(s))

    @pl.when(b < 7)
    def _():
        sig((c, b + 1, s))

    @pl.when(b > 0)
    def _():
        sig((c, b - 1, s))

    kept = (lax.broadcasted_iota(jnp.int32, (1, TXT), 1) < tlen[...].reshape(1, 1)) & (keep[...] == 1)
    mo[...] = jnp.broadcast_to(jnp.where(kept, 0.0, -1e30).astype(F32), (8, TXT))

    count = 18 + jnp.where(moved, 1, 0) + jnp.where(b < 7, 1, 0) + jnp.where(b > 0, 1, 0)
    pl.semaphore_wait(bar, count)

    rcvs = (rcv_q, rcv_k, rcv_v)

    def send_head(h):
        for kind in (1, 0, 2):
            landing = qb.at[h, 0, s] if kind == 0 else kv.at[h, 0, xl, kind - 1, s]

            def piece(d):
                return qkv.at[0, :, :, pl.ds(pl.multiple_of(kind * D + (d * G + h) * HD, HD), HD)]

            def one(j, carry):
                d = (s + j) % 8
                remote(piece(d), landing, snd.at[h, kind], rcvs[kind].at[h], peer(d)).start()
                return carry

            lax.fori_loop(1, 8, one, 0)

            @pl.when(moved)
            def _():
                remote(piece(s), landing, snd.at[h, kind], rcvs[kind].at[h], peer(s)).start()

            @pl.when(jnp.logical_not(moved))
            def _():
                pltpu.make_async_copy(piece(s), landing, rcvs[kind].at[h]).start()

    def share_keys(h, kind):
        mine = kv.at[h, 0, c, kind]
        wait_bytes(mine, (rcv_k, rcv_v)[kind].at[h])
        remote(mine, kv.at[h, 1, c, kind], ysnd.at[h, kind], yrcv.at[h, kind], to_k).start()
        remote(mine, mine, dsnd.at[h, 0, kind], drcv.at[h, 0, kind], to_core).start()

    def share_queries(h):
        wait_bytes(qb.at[h, 0], rcv_q.at[h])
        remote(qb.at[h, 0], qb.at[h, 1], qsnd.at[h], qrcv.at[h], to_q).start()

    def share(h):
        share_keys(h, 0)
        share_queries(h)
        share_keys(h, 1)

    def pass_far(h):
        for kind in range(2):
            far = kv.at[h, 1, c, kind]
            wait_bytes(far, yrcv.at[h, kind])
            remote(far, far, dsnd.at[h, 1, kind], drcv.at[h, 1, kind], to_core).start()

    def wait_core(h, far):
        for kind in range(2):
            wait_bytes(kv.at[h, far, 1 - c, kind], drcv.at[h, far, kind])

    fetch_t = pltpu.make_async_copy(text_kv.at[0], ta, lsem.at[3])
    mask_own = pltpu.make_async_copy(mo, mb.at[c], lsem.at[4])
    mask_out = remote(mo, mb.at[c], tsnd.at[1], trcv.at[1], to_core)

    def take_text(kind):
        def some(n, carry):
            tokens = pl.ds(pl.multiple_of(n * 32, 32), 32)
            found = ta[tokens, kind].astype(F32)
            head = lax.broadcasted_iota(jnp.int32, (32, H, HD), 1)
            for g in range(G):
                row = jnp.sum(jnp.where(head == s * G + g, found, 0.0), axis=1)
                tb[c, kind, g, tokens] = row.astype(BF)
            return carry

        lax.fori_loop(0, TXT // 32, some, 0)
        remote(tb.at[c, kind], tb.at[c, kind], xsnd.at[kind], xrcv.at[kind], to_core).start()

    fetch_t.start()
    send_head(0)
    mask_own.start()
    mask_out.start()
    send_head(1)
    fetch_t.wait()
    take_text(0)
    share_keys(0, 0)
    send_head(2)
    take_text(1)
    share_queries(0)
    share_keys(0, 1)
    fetch_w.start()
    fetch_r.start()
    fetch_f.start()

    blocks = 1024 // QB

    def place(u):
        return (u + s // 2) % blocks

    def rows_of(u):
        return pl.ds(pl.multiple_of(place(u) * QB, QB), QB)

    def queries(h, r, u):
        return qb[h, r, pl.ds(2 * place(u), 2)].reshape(QB, HD)

    def scores(q, keys):
        return lax.dot_general(q, keys, (((1,), (1,)), ((), ())), preferred_element_type=F32)

    def weigh(weights, values):
        padded = jnp.concatenate([values, jnp.ones_like(values)], axis=1)
        return jnp.dot(weights.astype(BF), padded, preferred_element_type=F32)

    def softmax_blocks(h, far, r, done=None):
        keys = kv[h, far, :, 0].reshape(-1, HD)
        values = kv[h, far, :, 1].reshape(-1, HD)
        with_text = far == 0 and r == 0
        if with_text:
            text_keys = tb[xl, 0, h]
            text_values = tb[xl, 1, h]
            added = mb[xl]

        def all_scores(u):
            q = queries(h, r, u)
            if not with_text:
                return scores(q, keys), None
            return scores(q, keys), scores(q, text_keys) + added[0:1]

        ahead = all_scores(0)
        for u in range(blocks):
            now, now_text = ahead
            if u + 1 < blocks:
                ahead = all_scores(u + 1)
            rows = rows_of(u)
            top = jnp.max(now, axis=1, keepdims=True)
            if far == 0:
                if with_text:
                    top = jnp.maximum(top, jnp.max(now_text, axis=1, keepdims=True))
                new = jnp.broadcast_to(top, (QB, HD))
                out = weigh(jnp.exp2((now - top) * SCALE), values)
                if with_text:
                    out = out + weigh(jnp.exp2((now_text - top) * SCALE), text_values)
                total, weight = out[:, :HD], out[:, HD:]
            else:
                old = m_s[r, rows]
                new = jnp.maximum(old, top)
                factor = jnp.exp2((old - new) * SCALE)
                out = weigh(jnp.exp2((now - new[:, :1]) * SCALE), values)
                total = acc[r, rows] * factor + out[:, :HD]
                weight = l_s[r, rows] * factor + out[:, HD:]
            if done is not None:
                done(u, new, total, weight)
            else:
                m_s[r, rows] = new
                acc[r, rows] = total
                l_s[r, rows] = weight

    def finish(h, r):
        def done(i, top, total, weight):
            out = (total / weight).astype(BF)
            lane = lax.broadcasted_iota(jnp.int32, (QB, HD), 1)
            stats = jnp.where(lane == 0, top, weight).T[0:8]
            high = stats.astype(BF)
            rest = stats - high.astype(F32)
            middle = rest.astype(BF)
            low = rest - middle.astype(F32)
            line = lax.broadcasted_iota(jnp.int32, (8, QB), 0)
            second = jnp.where(line == 2, low[0:1], middle.astype(F32))
            below = jnp.concatenate([high.astype(F32), second], axis=0).astype(BF)
            for k in range(2):
                d = 2 * place(i) + k
                ob[r, h, d, 0:ROWS] = out[k * ROWS : (k + 1) * ROWS]
                ob[r, h, d, ROWS : ROWS + 16] = below[:, k * ROWS : (k + 1) * ROWS]

        return done

    def send_out(h, r):
        def one(j, carry):
            d = (2 * (s // 2) + j) % 8
            slab = ob.at[r, h, d]
            landing = att.at[r, s, h]
            if r:
                remote(slab, landing, osnd.at[h, 1], orcv.at[h, 1], owner(1, d)).start()
                return carry

            @pl.when(jnp.logical_or(moved, d != s))
            def _():
                remote(slab, landing, osnd.at[h, 0], orcv.at[h, 0], owner(0, d)).start()

            @pl.when(jnp.logical_not(jnp.logical_or(moved, d != s)))
            def _():
                pltpu.make_async_copy(slab, landing, orcv.at[h, 0]).start()

            return carry

        lax.fori_loop(0, 8, one, 0)

    def project(h):
        tops, sums = [], []
        for r in range(2):
            wait_bytes(att.at[r, :, h], orcv.at[h, r])
            stats = att[r, :, h, ROWS : ROWS + 16].astype(F32)
            tops.append(stats[:, 0] + stats[:, 8] + stats[:, 10])
            sums.append(stats[:, 1] + stats[:, 9])
        top = jnp.maximum(tops[0], tops[1])
        parts = [jnp.exp2((tops[r] - top) * SCALE) * sums[r] for r in range(2)]
        whole = parts[0] + parts[1]
        shares = [(part / whole).T for part in parts]
        rows = jnp.concatenate(
            [
                sum(att[r, d, h, 0:ROWS].astype(F32) * shares[r][:, d : d + 1] for r in range(2)).astype(BF)
                for d in range(8)
            ],
            axis=1,
        )

        def columns(n, carry):
            cols = pl.ds(pl.multiple_of(n * 512, 512), 512)
            weight = jnp.concatenate(
                [wo[pl.ds(pl.multiple_of((d * G + h) * HD, HD), HD), cols] for d in range(8)], axis=0
            )
            proj[:, cols] += jnp.dot(rows, weight, preferred_element_type=F32)
            return carry

        lax.fori_loop(0, D // 512, columns, 0)

    proj[...] = jnp.zeros_like(proj)
    mask_own.wait()
    for kind in range(2):
        wait_bytes(tb.at[1 - c, kind], xrcv.at[kind])
    wait_bytes(mb.at[1 - c], trcv.at[1])

    def step(h, carry):
        wait_core(h, 0)
        softmax_blocks(h, 0, 0)

        @pl.when(h == 1)
        def _():
            share(2)

        @pl.when(h > 0)
        def _():
            pass_far(h)

        wait_bytes(qb.at[h, 1], qrcv.at[h])
        softmax_blocks(h, 0, 1)

        @pl.when(h == 0)
        def _():
            pass_far(0)
            share(1)

        wait_core(h, 1)
        softmax_blocks(h, 1, 1, finish(h, 1))
        send_out(h, 1)
        softmax_blocks(h, 1, 0, finish(h, 0))
        send_out(h, 0)
        return carry

    lax.fori_loop(0, G, step, 0)
    fetch_w.wait()
    project(0)
    project(1)

    def wait_out(h):
        wait_bytes(ob.at[1, h], osnd.at[h, 1])
        wait_bytes(ob.at[0, h, pl.ds(0, 7)], osnd.at[h, 0])

        @pl.when(moved)
        def _():
            wait_bytes(ob.at[0, h, 0], osnd.at[h, 0])

    for h in range(G):
        for kind in range(3):
            wait_bytes(qb.at[h, 0, pl.ds(0, 7)], snd.at[h, kind])

            @pl.when(moved)
            def _():
                wait_bytes(qb.at[h, 0, 0], snd.at[h, kind])

        wait_bytes(qb.at[h, 0], qsnd.at[h])
        for kind in range(2):
            wait_bytes(kv.at[h, 0, c, 0], ysnd.at[h, kind])
            for far in range(2):
                wait_bytes(kv.at[h, 0, c, 0], dsnd.at[h, far, kind])
    for kind in range(2):
        wait_bytes(tb.at[c, kind], xsnd.at[kind])
    wait_bytes(mb.at[c], tsnd.at[1])
    wait_out(0)
    wait_out(1)
    project(G - 1)

    fetch_r.wait()
    fetch_f.wait()

    def norm(n, carry):
        rows = pl.ds(pl.multiple_of(n * 32, 32), 32)
        shown = res[n // 2, pl.ds(pl.multiple_of((n % 2) * 32, 32), 32)].astype(F32)
        hidden = shown + gate[...] * proj[rows]
        centered = hidden - jnp.mean(hidden, axis=1, keepdims=True)
        normed = centered * lax.rsqrt(jnp.mean(centered * centered, axis=1, keepdims=True) + norm_eps)
        mod[rows] = (normed * (1.0 + fmod[0, 1:2]) + fmod[0, 0:1]).astype(BF)
        return carry

    lax.fori_loop(0, 4, norm, 0)
    pb[c] = lax.dot_general(mod[...], wf[...], (((1,), (1,)), ((), ())), preferred_element_type=F32)
    remote(pb.at[c], pb.at[c], gsnd, grcv, to_core).start()
    wait_bytes(pb.at[1 - c], grcv)
    uncond = pb[1]
    guided = uncond + guidance_scale * (pb[0] - uncond)
    guided_out[...] = guided
    lat[...] = ((noisy[...] - sigma_last * guided) / vae_factor).astype(BF)

    @pl.when(b < 7)
    def _():
        remote(lat, halo, hsnd, hrcv, (c, b + 1, s)).start()

    latents[1] = lat[...]

    @pl.when(b == 0)
    def _():
        latents[0] = jnp.zeros_like(halo)

    @pl.when(b > 0)
    def _():
        wait_bytes(halo, hrcv)
        latents[0] = halo[...]

    wait_out(2)
    wait_bytes(pb.at[c], gsnd)

    @pl.when(b < 7)
    def _():
        wait_bytes(lat, hsnd)


def conv_body(guided, latents, conv_w, conv_b, velocity, decoded):
    c = lax.axis_index("cfg")
    velocity[...] = guided[...].reshape(2, 64, 64)
    before = latents[0]
    here = latents[1]
    across = jnp.concatenate([before[64:], here[:64]], axis=0)
    entry = lax.broadcasted_iota(jnp.int32, (64, 48), 0)
    place = lax.broadcasted_iota(jnp.int32, (64, 48), 1)
    outs = []
    for i in range(2):
        taps = jnp.zeros((ROWS, 48), F32)
        for t, frames in enumerate((before, across, here)):
            chosen = (entry == 4 * (place - 16 * t) + 2 * c + i) & (place >= 16 * t) & (place < 16 * t + 16)
            taps = taps + jnp.dot(frames, jnp.where(chosen, 1.0, 0.0).astype(BF), preferred_element_type=F32)
        out = jnp.dot(taps.astype(BF), conv_w[...], preferred_element_type=F32) + conv_b[...]
        outs.append(out.reshape(2, 64, 512))
    decoded[...] = jnp.stack(outs, axis=2).astype(BF)


def shards(qkv, residual, text_kv, text_len, text_keep, attn_gate, w_out, final_mod, w_final, noisy, conv_weight, conv_bias):
    hbm = pl.BlockSpec(memory_space=pl.ANY)
    vmem = pl.BlockSpec(memory_space=pltpu.VMEM)
    dma = pltpu.SemaphoreType.DMA
    guided, latents = pl.pallas_call(
        body,
        out_shape=(
            jax.ShapeDtypeStruct((ROWS, 64), F32),
            jax.ShapeDtypeStruct((2, ROWS, 64), BF),
        ),
        in_specs=[hbm, hbm, hbm, vmem, vmem, vmem, hbm, vmem, hbm, vmem],
        out_specs=(vmem, vmem),
        scratch_shapes=[
            pltpu.VMEM((G, 2, 8, 2, 64, HD), BF),
            pltpu.VMEM((G, 2, 2, 2, 8, 2, 64, HD), BF),
            pltpu.VMEM((2, G, 8, ROWS + 16, HD), BF),
            pltpu.VMEM((2, 8, G, ROWS + 16, HD), BF),
            pltpu.VMEM((TXT, 2, H, HD), BF),
            pltpu.VMEM((2, 2, G, TXT, HD), BF),
            pltpu.VMEM((8, TXT), F32),
            pltpu.VMEM((2, 8, TXT), F32),
            pltpu.VMEM((D, D), BF),
            pltpu.VMEM((2, 64, D), BF),
            pltpu.VMEM((64, D), BF),
            pltpu.VMEM((ROWS, D), F32),
            pltpu.VMEM((ROWS, D), BF),
            pltpu.VMEM((2, ROWS, 64), F32),
            pltpu.VMEM((ROWS, 64), BF),
            pltpu.VMEM((ROWS, 64), BF),
            pltpu.VMEM((2, 1024, HD), F32),
            pltpu.VMEM((2, 1024, HD), F32),
            pltpu.VMEM((2, 1024, HD), F32),
            dma((G, 3)),
            dma((G,)),
            dma((G,)),
            dma((G,)),
            dma((G, 2)),
            dma((G, 2)),
            dma((G,)),
            dma((G,)),
            dma((G, 2, 2)),
            dma((G, 2, 2)),
            dma((G, 2)),
            dma((G, 2)),
            dma((5,)),
            dma((2,)),
            dma((2,)),
            dma((2,)),
            dma((2,)),
            dma,
            dma,
            dma,
            dma,
        ],
        compiler_params=pltpu.CompilerParams(
            collective_id=0, has_side_effects=True, vmem_limit_bytes=60 * 2**20
        ),
    )(
        qkv,
        residual,
        text_kv,
        text_len,
        text_keep,
        attn_gate,
        w_out,
        final_mod,
        w_final.T,
        noisy.reshape(ROWS, 64),
    )
    return pl.pallas_call(
        conv_body,
        out_shape=(
            jax.ShapeDtypeStruct((2, 64, 64), F32),
            jax.ShapeDtypeStruct((2, 64, 2, 512), BF),
        ),
        in_specs=[vmem] * 4,
        out_specs=(vmem, vmem),
    )(guided, latents, conv_weight.reshape(48, 512), conv_bias.reshape(1, 512))


def solution(mesh):
    return jax.shard_map(
        shards,
        mesh=mesh,
        in_specs=(
            P("cfg", "blk", "sp", None),
            P("cfg", "blk", "sp", None),
            P("cfg", None, None, None, None),
            P("cfg"),
            P("cfg", None),
            P("cfg", None),
            P(),
            P("cfg", None, None),
            P(),
            P("blk", "sp", None),
            P(),
            P(),
        ),
        out_specs=(P("blk", "sp", None), P("blk", "sp", "cfg", None)),
        check_vma=False,
    )
```

```python
import functools
import math

import jax
import jax.numpy as jnp
from jax import lax
from jax.experimental import pallas as pl
from jax.experimental.pallas import tpu as pltpu
from jax.sharding import PartitionSpec as P

D = 3072
H = 24
HD = 128
G = 3
TXT = 256
ROWS = 128
QB = 256
MESH = pl.DeviceIdType.MESH
SCALE = math.log2(math.e) / math.sqrt(HD)
BF = jnp.bfloat16
F32 = jnp.float32

guidance_scale = 6.0
sigma_last = 0.125
vae_factor = 0.476986
norm_eps = 1e-06


def wait_bytes(ref, sem):
    pltpu.make_async_copy(ref, ref, sem).wait()


def body(
    qkv, residual, text_kv, tlen, keep, gate, w_out, fmod, w_fin, noisy,
    guided_out, latents,
    qb, kv, ob, att, ta, tb, mo, mb, wo, res, wf, proj, mod, pb, lat, halo, acc, m_s, l_s,
    snd, rcv_q, rcv_k, rcv_v, ysnd, yrcv, qsnd, qrcv, dsnd, drcv, osnd, orcv, lsem, tsnd, trcv, xsnd, xrcv, gsnd, grcv, hsnd, hrcv,
):
    c = lax.axis_index("cfg")
    b = lax.axis_index("blk")
    s = lax.axis_index("sp")
    xl = b // 4
    y = b % 4
    yq = y + 1 - 2 * (y % 2)
    to_q = (c, xl * 4 + yq, s)
    to_k = (c, xl * 4 + 3 - y, s)
    to_core = (1 - c, b, s)
    moved = c != xl

    def peer(d):
        return (xl, c * 4 + y, d)

    def owner(r, d):
        return (xl, c * 4 + (yq if r else y), d)

    def remote(src, dst, send, recv, dev):
        return pltpu.make_async_remote_copy(src, dst, send, recv, device_id=dev, device_id_type=MESH)

    fetch_w = pltpu.make_async_copy(w_out, wo, lsem.at[0])
    fetch_r = pltpu.make_async_copy(residual.at[0], res, lsem.at[1])
    fetch_f = pltpu.make_async_copy(w_fin, wf, lsem.at[2])

    bar = pltpu.get_barrier_semaphore()

    def sig(dev):
        pl.semaphore_signal(bar, inc=1, device_id=dev, device_id_type=MESH)

    sig(to_q)
    sig(to_k)
    sig(to_core)
    for j in range(1, 8):
        sig(peer((s + j) % 8))
    for j in range(8):
        sig(owner(1, (s + j) % 8))

    @pl.when(moved)
    def _():
        sig(peer(s))

    @pl.when(b < 7)
    def _():
        sig((c, b + 1, s))

    @pl.when(b > 0)
    def _():
        sig((c, b - 1, s))

    kept = (lax.broadcasted_iota(jnp.int32, (1, TXT), 1) < tlen[...].reshape(1, 1)) & (keep[...] == 1)
    mo[...] = jnp.broadcast_to(jnp.where(kept, 0.0, -1e30).astype(F32), (8, TXT))

    count = 18 + jnp.where(moved, 1, 0) + jnp.where(b < 7, 1, 0) + jnp.where(b > 0, 1, 0)
    pl.semaphore_wait(bar, count)

    rcvs = (rcv_q, rcv_k, rcv_v)

    def send_head(h):
        for kind in (1, 0, 2):
            landing = qb.at[h, 0, s] if kind == 0 else kv.at[h, 0, xl, kind - 1, s]

            def piece(d):
                return qkv.at[0, :, :, pl.ds(pl.multiple_of(kind * D + (d * G + h) * HD, HD), HD)]

            def one(j, carry):
                d = (s + j) % 8
                remote(piece(d), landing, snd.at[h, kind], rcvs[kind].at[h], peer(d)).start()
                return carry

            lax.fori_loop(1, 8, one, 0)

            @pl.when(moved)
            def _():
                remote(piece(s), landing, snd.at[h, kind], rcvs[kind].at[h], peer(s)).start()

            @pl.when(jnp.logical_not(moved))
            def _():
                pltpu.make_async_copy(piece(s), landing, rcvs[kind].at[h]).start()

    def share_keys(h, kind):
        mine = kv.at[h, 0, c, kind]
        wait_bytes(mine, (rcv_k, rcv_v)[kind].at[h])
        remote(mine, kv.at[h, 1, c, kind], ysnd.at[h, kind], yrcv.at[h, kind], to_k).start()
        remote(mine, mine, dsnd.at[h, 0, kind], drcv.at[h, 0, kind], to_core).start()

    def share_queries(h):
        wait_bytes(qb.at[h, 0], rcv_q.at[h])
        remote(qb.at[h, 0], qb.at[h, 1], qsnd.at[h], qrcv.at[h], to_q).start()

    def share(h):
        share_keys(h, 0)
        share_queries(h)
        share_keys(h, 1)

    def pass_far(h):
        for kind in range(2):
            far = kv.at[h, 1, c, kind]
            wait_bytes(far, yrcv.at[h, kind])
            remote(far, far, dsnd.at[h, 1, kind], drcv.at[h, 1, kind], to_core).start()

    def wait_core(h, far):
        for kind in range(2):
            wait_bytes(kv.at[h, far, 1 - c, kind], drcv.at[h, far, kind])

    fetch_t = pltpu.make_async_copy(text_kv.at[0], ta, lsem.at[3])
    mask_own = pltpu.make_async_copy(mo, mb.at[c], lsem.at[4])
    mask_out = remote(mo, mb.at[c], tsnd.at[1], trcv.at[1], to_core)

    def take_text(kind):
        def some(n, carry):
            tokens = pl.ds(pl.multiple_of(n * 32, 32), 32)
            found = ta[tokens, kind].astype(F32)
            head = lax.broadcasted_iota(jnp.int32, (32, H, HD), 1)
            for g in range(G):
                row = jnp.sum(jnp.where(head == s * G + g, found, 0.0), axis=1)
                tb[c, kind, g, tokens] = row.astype(BF)
            return carry

        lax.fori_loop(0, TXT // 32, some, 0)
        remote(tb.at[c, kind], tb.at[c, kind], xsnd.at[kind], xrcv.at[kind], to_core).start()

    fetch_t.start()
    send_head(0)
    mask_own.start()
    mask_out.start()
    send_head(1)
    fetch_t.wait()
    take_text(0)
    share_keys(0, 0)
    send_head(2)
    take_text(1)
    share_queries(0)
    share_keys(0, 1)
    fetch_w.start()
    fetch_r.start()
    fetch_f.start()

    blocks = 1024 // QB

    def place(u):
        return (u + s // 2) % blocks

    def rows_of(u):
        return pl.ds(pl.multiple_of(place(u) * QB, QB), QB)

    def queries(h, r, u):
        return qb[h, r, pl.ds(2 * place(u), 2)].reshape(QB, HD)

    def scores(q, keys):
        return lax.dot_general(q, keys, (((1,), (1,)), ((), ())), preferred_element_type=F32)

    def weigh(weights, values):
        padded = jnp.concatenate([values, jnp.ones_like(values)], axis=1)
        return jnp.dot(weights.astype(BF), padded, preferred_element_type=F32)

    def softmax_blocks(h, far, r, done=None):
        keys = kv[h, far, :, 0].reshape(-1, HD)
        values = kv[h, far, :, 1].reshape(-1, HD)
        with_text = far == 0 and r == 0
        if with_text:
            text_keys = tb[xl, 0, h]
            text_values = tb[xl, 1, h]
            added = mb[xl]

        def all_scores(u):
            q = queries(h, r, u)
            if not with_text:
                return scores(q, keys), None
            return scores(q, keys), scores(q, text_keys) + added[0:1]

        ahead = all_scores(0)
        for u in range(blocks):
            now, now_text = ahead
            if u + 1 < blocks:
                ahead = all_scores(u + 1)
            rows = rows_of(u)
            top = jnp.max(now, axis=1, keepdims=True)
            if far == 0:
                if with_text:
                    top = jnp.maximum(top, jnp.max(now_text, axis=1, keepdims=True))
                new = jnp.broadcast_to(top, (QB, HD))
                out = weigh(jnp.exp2((now - top) * SCALE), values)
                if with_text:
                    out = out + weigh(jnp.exp2((now_text - top) * SCALE), text_values)
                total, weight = out[:, :HD], out[:, HD:]
            else:
                old = m_s[r, rows]
                new = jnp.maximum(old, top)
                factor = jnp.exp2((old - new) * SCALE)
                out = weigh(jnp.exp2((now - new[:, :1]) * SCALE), values)
                total = acc[r, rows] * factor + out[:, :HD]
                weight = l_s[r, rows] * factor + out[:, HD:]
            if done is not None:
                done(u, new, total, weight)
            else:
                m_s[r, rows] = new
                acc[r, rows] = total
                l_s[r, rows] = weight

    def finish(h, r):
        def done(i, top, total, weight):
            out = (total / weight).astype(BF)
            lane = lax.broadcasted_iota(jnp.int32, (QB, HD), 1)
            stats = jnp.where(lane == 0, top, weight).T[0:8]
            high = stats.astype(BF)
            rest = stats - high.astype(F32)
            middle = rest.astype(BF)
            low = rest - middle.astype(F32)
            line = lax.broadcasted_iota(jnp.int32, (8, QB), 0)
            second = jnp.where(line == 2, low[0:1], middle.astype(F32))
            below = jnp.concatenate([high.astype(F32), second], axis=0).astype(BF)
            for k in range(2):
                d = 2 * place(i) + k
                ob[r, h, d, 0:ROWS] = out[k * ROWS : (k + 1) * ROWS]
                ob[r, h, d, ROWS : ROWS + 16] = below[:, k * ROWS : (k + 1) * ROWS]

        return done

    def send_out(h, r):
        def one(j, carry):
            d = (2 * (s // 2) + j) % 8
            slab = ob.at[r, h, d]
            landing = att.at[r, s, h]
            if r:
                remote(slab, landing, osnd.at[h, 1], orcv.at[h, 1], owner(1, d)).start()
                return carry

            @pl.when(jnp.logical_or(moved, d != s))
            def _():
                remote(slab, landing, osnd.at[h, 0], orcv.at[h, 0], owner(0, d)).start()

            @pl.when(jnp.logical_not(jnp.logical_or(moved, d != s)))
            def _():
                pltpu.make_async_copy(slab, landing, orcv.at[h, 0]).start()

            return carry

        lax.fori_loop(0, 8, one, 0)

    def project(h):
        tops, sums = [], []
        for r in range(2):
            wait_bytes(att.at[r, :, h], orcv.at[h, r])
            stats = att[r, :, h, ROWS : ROWS + 16].astype(F32)
            tops.append(stats[:, 0] + stats[:, 8] + stats[:, 10])
            sums.append(stats[:, 1] + stats[:, 9])
        top = jnp.maximum(tops[0], tops[1])
        parts = [jnp.exp2((tops[r] - top) * SCALE) * sums[r] for r in range(2)]
        whole = parts[0] + parts[1]
        shares = [(part / whole).T for part in parts]
        rows = jnp.concatenate(
            [
                sum(att[r, d, h, 0:ROWS].astype(F32) * shares[r][:, d : d + 1] for r in range(2)).astype(BF)
                for d in range(8)
            ],
            axis=1,
        )

        def columns(n, carry):
            cols = pl.ds(pl.multiple_of(n * 512, 512), 512)
            weight = jnp.concatenate(
                [wo[pl.ds(pl.multiple_of((d * G + h) * HD, HD), HD), cols] for d in range(8)], axis=0
            )
            proj[:, cols] += jnp.dot(rows, weight, preferred_element_type=F32)
            return carry

        lax.fori_loop(0, D // 512, columns, 0)

    proj[...] = jnp.zeros_like(proj)
    mask_own.wait()
    for kind in range(2):
        wait_bytes(tb.at[1 - c, kind], xrcv.at[kind])
    wait_bytes(mb.at[1 - c], trcv.at[1])

    def step(h, carry):
        wait_core(h, 0)
        softmax_blocks(h, 0, 0)

        @pl.when(h == 1)
        def _():
            share(2)

        @pl.when(h > 0)
        def _():
            pass_far(h)

        wait_bytes(qb.at[h, 1], qrcv.at[h])
        softmax_blocks(h, 0, 1)

        @pl.when(h == 0)
        def _():
            pass_far(0)
            share(1)

        wait_core(h, 1)
        softmax_blocks(h, 1, 1, finish(h, 1))
        send_out(h, 1)
        softmax_blocks(h, 1, 0, finish(h, 0))
        send_out(h, 0)
        return carry

    lax.fori_loop(0, G, step, 0)
    fetch_w.wait()
    project(0)
    project(1)

    def wait_out(h):
        wait_bytes(ob.at[1, h], osnd.at[h, 1])
        wait_bytes(ob.at[0, h, pl.ds(0, 7)], osnd.at[h, 0])

        @pl.when(moved)
        def _():
            wait_bytes(ob.at[0, h, 0], osnd.at[h, 0])

    for h in range(G):
        for kind in range(3):
            wait_bytes(qb.at[h, 0, pl.ds(0, 7)], snd.at[h, kind])

            @pl.when(moved)
            def _():
                wait_bytes(qb.at[h, 0, 0], snd.at[h, kind])

        wait_bytes(qb.at[h, 0], qsnd.at[h])
        for kind in range(2):
            wait_bytes(kv.at[h, 0, c, 0], ysnd.at[h, kind])
            for far in range(2):
                wait_bytes(kv.at[h, 0, c, 0], dsnd.at[h, far, kind])
    for kind in range(2):
        wait_bytes(tb.at[c, kind], xsnd.at[kind])
    wait_bytes(mb.at[c], tsnd.at[1])
    wait_out(0)
    wait_out(1)
    project(G - 1)

    fetch_r.wait()
    fetch_f.wait()

    def norm(n, carry):
        rows = pl.ds(pl.multiple_of(n * 32, 32), 32)
        shown = res[n // 2, pl.ds(pl.multiple_of((n % 2) * 32, 32), 32)].astype(F32)
        hidden = shown + gate[...] * proj[rows]
        centered = hidden - jnp.mean(hidden, axis=1, keepdims=True)
        normed = centered * lax.rsqrt(jnp.mean(centered * centered, axis=1, keepdims=True) + norm_eps)
        mod[rows] = (normed * (1.0 + fmod[0, 1:2]) + fmod[0, 0:1]).astype(BF)
        return carry

    lax.fori_loop(0, 4, norm, 0)
    pb[c] = lax.dot_general(mod[...], wf[...], (((1,), (1,)), ((), ())), preferred_element_type=F32)
    remote(pb.at[c], pb.at[c], gsnd, grcv, to_core).start()
    wait_bytes(pb.at[1 - c], grcv)
    uncond = pb[1]
    guided = uncond + guidance_scale * (pb[0] - uncond)
    guided_out[...] = guided
    lat[...] = ((noisy[...] - sigma_last * guided) / vae_factor).astype(BF)

    @pl.when(b < 7)
    def _():
        remote(lat, halo, hsnd, hrcv, (c, b + 1, s)).start()

    latents[1] = lat[...]

    @pl.when(b == 0)
    def _():
        latents[0] = jnp.zeros_like(halo)

    @pl.when(b > 0)
    def _():
        wait_bytes(halo, hrcv)
        latents[0] = halo[...]

    wait_out(2)
    wait_bytes(pb.at[c], gsnd)

    @pl.when(b < 7)
    def _():
        wait_bytes(lat, hsnd)


def conv_body(guided, latents, conv_w, conv_b, velocity, decoded):
    c = lax.axis_index("cfg")
    velocity[...] = guided[...].reshape(2, 64, 64)
    before = latents[0]
    here = latents[1]
    across = jnp.concatenate([before[64:], here[:64]], axis=0)
    entry = lax.broadcasted_iota(jnp.int32, (64, 48), 0)
    place = lax.broadcasted_iota(jnp.int32, (64, 48), 1)
    outs = []
    for i in range(2):
        taps = jnp.zeros((ROWS, 48), F32)
        for t, frames in enumerate((before, across, here)):
            chosen = (entry == 4 * (place - 16 * t) + 2 * c + i) & (place >= 16 * t) & (place < 16 * t + 16)
            taps = taps + jnp.dot(frames, jnp.where(chosen, 1.0, 0.0).astype(BF), preferred_element_type=F32)
        out = jnp.dot(taps.astype(BF), conv_w[...], preferred_element_type=F32) + conv_b[...]
        outs.append(out.reshape(2, 64, 512))
    decoded[...] = jnp.stack(outs, axis=2).astype(BF)


def shards(qkv, residual, text_kv, text_len, text_keep, attn_gate, w_out, final_mod, w_final, noisy, conv_weight, conv_bias):
    hbm = pl.BlockSpec(memory_space=pl.ANY)
    vmem = pl.BlockSpec(memory_space=pltpu.VMEM)
    dma = pltpu.SemaphoreType.DMA
    guided, latents = pl.pallas_call(
        body,
        out_shape=(
            pltpu.VMEM((ROWS, 64), F32),
            pltpu.VMEM((2, ROWS, 64), BF),
        ),
        in_specs=[hbm, hbm, hbm, vmem, vmem, vmem, hbm, vmem, hbm, vmem],
        out_specs=(vmem, vmem),
        scratch_shapes=[
            pltpu.VMEM((G, 2, 8, 2, 64, HD), BF),
            pltpu.VMEM((G, 2, 2, 2, 8, 2, 64, HD), BF),
            pltpu.VMEM((2, G, 8, ROWS + 16, HD), BF),
            pltpu.VMEM((2, 8, G, ROWS + 16, HD), BF),
            pltpu.VMEM((TXT, 2, H, HD), BF),
            pltpu.VMEM((2, 2, G, TXT, HD), BF),
            pltpu.VMEM((8, TXT), F32),
            pltpu.VMEM((2, 8, TXT), F32),
            pltpu.VMEM((D, D), BF),
            pltpu.VMEM((2, 64, D), BF),
            pltpu.VMEM((64, D), BF),
            pltpu.VMEM((ROWS, D), F32),
            pltpu.VMEM((ROWS, D), BF),
            pltpu.VMEM((2, ROWS, 64), F32),
            pltpu.VMEM((ROWS, 64), BF),
            pltpu.VMEM((ROWS, 64), BF),
            pltpu.VMEM((2, 1024, HD), F32),
            pltpu.VMEM((2, 1024, HD), F32),
            pltpu.VMEM((2, 1024, HD), F32),
            dma((G, 3)),
            dma((G,)),
            dma((G,)),
            dma((G,)),
            dma((G, 2)),
            dma((G, 2)),
            dma((G,)),
            dma((G,)),
            dma((G, 2, 2)),
            dma((G, 2, 2)),
            dma((G, 2)),
            dma((G, 2)),
            dma((5,)),
            dma((2,)),
            dma((2,)),
            dma((2,)),
            dma((2,)),
            dma,
            dma,
            dma,
            dma,
        ],
        compiler_params=pltpu.CompilerParams(
            collective_id=0, has_side_effects=True, vmem_limit_bytes=60 * 2**20
        ),
    )(
        qkv,
        residual,
        text_kv,
        text_len,
        text_keep,
        attn_gate,
        w_out,
        final_mod,
        w_final.T,
        noisy.reshape(ROWS, 64),
    )
    return pl.pallas_call(
        conv_body,
        out_shape=(
            jax.ShapeDtypeStruct((2, 64, 64), F32),
            jax.ShapeDtypeStruct((2, 64, 2, 512), BF),
        ),
        in_specs=[vmem] * 4,
        out_specs=(vmem, vmem),
    )(guided, latents, conv_weight.reshape(48, 512), conv_bias.reshape(1, 512))


def solution(mesh):
    return jax.shard_map(
        shards,
        mesh=mesh,
        in_specs=(
            P("cfg", "blk", "sp", None),
            P("cfg", "blk", "sp", None),
            P("cfg", None, None, None, None),
            P("cfg"),
            P("cfg", None),
            P("cfg", None),
            P(),
            P("cfg", None, None),
            P(),
            P("blk", "sp", None),
            P(),
            P(),
        ),
        out_specs=(P("blk", "sp", None), P("blk", "sp", "cfg", None)),
        check_vma=False,
    )
```
